32 devices in a mesh: src: 8 (over z, y), dst: 4 (over x, core).
Axes of the slice: x: 2, y: 2, z: 4, core: 2. Of those that a mesh axis runs over, the one named last changes fastest.
Arguments:
- features: bfloat16 [4096, 128], P(('src', 'dst')), may hold values from -6 to 6
- weight: bfloat16 [128, 256], replicated, may hold values from -0.5 to 0.5
- bias: float32 [256], replicated, may hold values from -3 to 3
- tile_index: int32 [8, 4, 8], P('src', 'dst'), may hold values from 0 to 31, as said below
- edge_count: int32 [8, 4, 8], P('src', 'dst'), may hold values from 0 to 64, as said below
- edge_pos: int32 [8, 4, 8, 64], P('src', 'dst'), may hold values from 0 to 16383
- edge_weight: bfloat16 [8, 4, 8, 64], P('src', 'dst'), may hold values from 0.099609375 to 0.3984375
- grad_out: bfloat16 [4096, 256], P(('src', 'dst')), may hold values from -15 to 15
Outputs:
- hidden: bfloat16 [4096, 256], P(('src', 'dst'))
- input_grad: bfloat16 [4096, 128], P(('src', 'dst'))
- weight_grad: float32 [128, 256], replicated
- bias_grad: float32 [256], replicated
The draws below stay inside these ranges and needn't reach their ends.
Inputs may be any that keep to these rules, and one draw needn't show every extreme that they name: `tile_index`: the 8 entries of one device are distinct; id c names tile row c // 4 and tile column c % 4 of the device's block of 1024 target rows and 512 source columns. `edge_count`: on each device the live slots (count 1 or more) come first and all later slots have count 0; slot 0 is always live; some device has all 8 slots live; every device has a slot with 64 edges. `edge_pos`: row * 128 + column inside the tile; positions may repeat within a tile.
All inputs are finite; a program needn't handle non-finite values.
Results may differ from the reference program's by a relative error of at most 0.0065.
Values may be sent and summed in bfloat16 or wider, within the bound.
A program may use at most 64 MiB of HBM per device.

```python
import math
import jax
import jax.numpy as jnp
from jax import lax

F_IN = 128
F_HID = 256
NODE_DEV = 128
TILE = 128
EDGE_TILE = 64
SRC_ROWS = 512
SRC_TILES = 4
DST_TILES = 8
TILES_DEV = 8
NODES = 4096
N_SRC = 8
N_DST = 4


def live_tiles(key):
    first_draw = jax.random.randint(jax.random.fold_in(key, 11), (N_SRC, N_DST), 0, TILES_DEV + 1)
    second = jax.random.randint(jax.random.fold_in(key, 12), (N_SRC, N_DST), 0, TILES_DEV + 1)
    live_count = jnp.maximum(max(TILES_DEV // 8, 1), first_draw * second // TILES_DEV)
    busiest = jax.random.randint(jax.random.fold_in(key, 13), (), 0, N_SRC * N_DST)
    flat_live = live_count.reshape(-1)
    flat_live = jnp.where(jnp.arange(N_SRC * N_DST, dtype=jnp.int32) == busiest, TILES_DEV, flat_live)
    return flat_live.reshape(N_SRC, N_DST)


def draw_tile_index(key, part):
    slot_total = SRC_TILES * DST_TILES
    scores = jax.random.randint(key, (N_SRC, N_DST, slot_total), 0, 1 << 16) * slot_total + jnp.arange(slot_total, dtype=jnp.int32)
    ordering = jnp.argsort(scores, axis=-1)
    return ordering[:, :, :TILES_DEV].astype(jnp.int32)


def draw_edge_count(key, part):
    live_count = live_tiles(key)
    counts = jax.random.randint(jax.random.fold_in(key, 21), (N_SRC, N_DST, TILES_DEV), 1, EDGE_TILE + 1)
    fullest = jax.random.randint(jax.random.fold_in(key, 22), (N_SRC, N_DST), 0, 1 << 20) % live_count
    slot_ids = jnp.arange(TILES_DEV, dtype=jnp.int32)
    counts = jnp.where(slot_ids[None, None, :] == fullest[:, :, None], EDGE_TILE, counts)
    return jnp.where(slot_ids[None, None, :] < live_count[:, :, None], counts, 0).astype(jnp.int32)


def draw_grad_out(key, part):
    row_ramp = jnp.exp(jnp.log(3.0) * jnp.arange(NODES, dtype=jnp.float32) / (NODES - 1))
    values = jnp.clip(jax.random.normal(key, (NODES, F_HID), jnp.float32), -5.0, 5.0)
    return (values * row_ramp[:, None]).astype(jnp.bfloat16)


def place_ends(values, key, least, high):
    longest = values.shape.index(max(values.shape))
    spots = []
    for shift in (0, 1):
        where = [jax.random.randint(jax.random.fold_in(key, axis), (), 0, length) for axis, length in enumerate(values.shape)]
        where[longest] = (where[longest] + shift) % values.shape[longest]
        spots.append(tuple(where))
    return values.at[spots[0]].set(least).at[spots[1]].set(high)


def shard_levels(rng, dims, shards, smallest, largest):
    def one(dim, blocks):
        draws = jax.random.uniform(jax.random.fold_in(jax.random.fold_in(rng, 6), dim), (blocks,), jnp.float32, smallest / len(shards), largest / len(shards))
        return jnp.repeat(jnp.exp(draws), dims[dim] // blocks).reshape((-1,) + (1,) * (len(dims) - dim - 1))

    loudness = one(*shards[0])
    for cut in shards[1:]:
        loudness = loudness * one(*cut)
    return loudness


def noise(stream_key, dims, spread, reach, split=(), kind=jnp.bfloat16):
    values = spread * jax.random.normal(stream_key, dims, jnp.float32)
    if split:
        values = values * shard_levels(stream_key, dims, split, -0.22, 0.18)
    return jnp.clip(values, -reach, reach).astype(kind)


def setup_inputs(seed: int = 0) -> dict:
    keys = jax.random.split(jax.random.key(seed), 9)
    features = noise(keys[0], (NODES, F_IN), 1.0, 6.0, ((0, 32),))
    weight = noise(keys[1], (F_IN, F_HID), F_IN ** -0.5, 0.5)
    bias = noise(keys[2], (F_HID,), 0.5, 3.0, (), jnp.float32)
    tile_index = draw_tile_index(jax.random.fold_in(keys[8], 71), 0)
    edge_count = draw_edge_count(jax.random.fold_in(keys[8], 71), 0)
    edge_pos = place_ends(jax.random.randint(keys[5], (N_SRC, N_DST, TILES_DEV, EDGE_TILE), 0, TILE * TILE), jax.random.fold_in(keys[5], 1), 0, (TILE * TILE) - 1).astype(jnp.int32)
    edge_weight = jnp.clip(jnp.exp(math.log(0.3984375) - 1.3862944 * jax.random.uniform(keys[6], (N_SRC, N_DST, TILES_DEV, EDGE_TILE), jnp.float32) ** shard_levels(keys[6], (N_SRC, N_DST, TILES_DEV, EDGE_TILE), ((0, 8), (1, 4)), -0.2, 0.2)), 0.099609375, 0.3984375).astype(jnp.bfloat16)
    grad_out = draw_grad_out(jax.random.fold_in(keys[8], 71), 0)
    return dict(features=features, weight=weight, bias=bias, tile_index=tile_index, edge_count=edge_count, edge_pos=edge_pos, edge_weight=edge_weight, grad_out=grad_out)


def edge_values(positions, weights, counts):
    slot_ids = jnp.arange(positions.shape[1], dtype=jnp.int32)
    live_mask = slot_ids[None, :] < counts[:, None]
    paired = (positions[:, :, None] == positions[:, None, :]) & live_mask[:, :, None] & live_mask[:, None, :]
    summed = lax.optimization_barrier(jnp.sum(jnp.where(paired, weights.astype(jnp.float32)[:, None, :], jnp.zeros((), jnp.float32)), axis=2))
    repeated = jnp.any(paired & (slot_ids[None, :, None] > slot_ids[None, None, :]), axis=2)
    rounded = lax.optimization_barrier(summed.astype(jnp.bfloat16)).astype(jnp.float32)
    return jnp.where(live_mask & jnp.logical_not(repeated), rounded, jnp.zeros((), jnp.float32))

def device_edges(device_index, tile_index, edge_count, edge_pos, edge_weight):
    src_part = device_index // N_DST
    dst_part = device_index % N_DST
    tile_ids = tile_index.reshape(-1, TILES_DEV)[device_index]
    counts = edge_count.reshape(-1, TILES_DEV)[device_index]
    positions = edge_pos.reshape(-1, TILES_DEV, EDGE_TILE)[device_index]
    weights = edge_weight.reshape(-1, TILES_DEV, EDGE_TILE)[device_index]
    values = edge_values(positions, weights, counts)
    local_source = (tile_ids % SRC_TILES)[:, None] * TILE + positions % TILE
    local_target = (tile_ids // SRC_TILES)[:, None] * TILE + positions // TILE
    sources = src_part * SRC_ROWS + local_source
    targets = local_target // NODE_DEV * SRC_ROWS + dst_part * NODE_DEV + local_target % NODE_DEV
    return (sources.reshape(-1).astype(jnp.int32), targets.reshape(-1).astype(jnp.int32), values.reshape(-1))

def reference(features, weight, bias, tile_index, edge_count, edge_pos, edge_weight, grad_out):
    device_ids = jnp.arange(N_SRC * N_DST, dtype=jnp.int32)
    source_values = features.astype(jnp.float32)

    def forward_step(running, device_index):
        sources, targets, values = device_edges(device_index, tile_index, edge_count, edge_pos, edge_weight)
        return (running.at[targets].add(values[:, None] * source_values[sources]), None)
    summed, _ = lax.scan(forward_step, jnp.zeros((NODES, F_IN), jnp.float32), device_ids)
    aggregated = summed.astype(jnp.bfloat16)
    preact = jnp.dot(aggregated, weight, preferred_element_type=jnp.float32) + bias
    hidden = jax.nn.silu(preact).astype(jnp.bfloat16)
    sigmoid_pre = jax.nn.sigmoid(preact)
    grad_pre = (grad_out.astype(jnp.float32) * sigmoid_pre * (1.0 + preact * (1.0 - sigmoid_pre))).astype(jnp.bfloat16)
    node_scale = 1.0 / math.sqrt(NODES)
    weight_grad = jnp.dot(aggregated.T, grad_pre, preferred_element_type=jnp.float32) * node_scale
    bias_grad = lax.optimization_barrier(jnp.sum(grad_pre.astype(jnp.float32), axis=0)) * node_scale
    back_rows = jnp.dot(grad_pre, weight.T, preferred_element_type=jnp.float32).astype(jnp.bfloat16)
    back_values = back_rows.astype(jnp.float32)

    def backward_step(running, device_index):
        sources, targets, values = device_edges(device_index, tile_index, edge_count, edge_pos, edge_weight)
        return (running.at[sources].add(values[:, None] * back_values[targets]), None)
    back_summed, _ = lax.scan(backward_step, jnp.zeros((NODES, F_IN), jnp.float32), device_ids)
    input_grad = back_summed.astype(jnp.bfloat16)
    return (hidden, input_grad, weight_grad, bias_grad)
```

```python
import functools
import math

import jax
import jax.numpy as jnp
from jax import lax
from jax.experimental import pallas as pl
from jax.experimental.pallas import tpu as pltpu
from jax.sharding import PartitionSpec as P

TILE = 128
F_IN = 128
F_HID = 256
UNITS = 32
NT = (((1,), (1,)), ((), ()))
F32 = jnp.float32
BF16 = jnp.bfloat16


def flip(me, k):
    out = me
    bit = 1
    while bit <= k:
        if k & bit:
            out = out + bit * (1 - 2 * (lax.div(me, bit) % 2))
        bit *= 2
    return out


def each_peer(n, me, body, order=None):
    if n <= 8 and n & (n - 1) == 0:
        for k in order or range(n - 1, 0, -1):
            body(k, flip(me, k))
    else:

        def step(k, carry):
            body(k, lax.rem(me + k, n))
            return carry

        lax.fori_loop(1, n, step, 0)


def rows(i, n=TILE):
    return pl.ds(pl.multiple_of(i * n, n), n)


def kernel(
    n_src, n_dst, slots, edges,
    tid_ref, cnt_ref, x_ref, w_ref, b_ref, pos_ref, ew_ref, go_ref,
    hid_ref, ig_ref, wg_ref, bg_ref,
    xs, rt, ct, adj, adjt, bsend, brecv, gall, fsend, frecv,
    wsend, wrecv, drecv, wfin,
    xss, xrs, bss, brs, gss, grs, fss, frs, wss, wrs, dss, drs, ass, ars,
):
    me_s = lax.axis_index("src")
    me_d = lax.axis_index("dst")
    per = UNITS // n_src
    src_peers = functools.partial(each_peer, n_src, me_s)
    dst_peers = functools.partial(each_peer, n_dst, me_d)

    def to_src(s, src, dst, ss, rs):
        return pltpu.make_async_remote_copy(
            src_ref=src, dst_ref=dst, send_sem=ss, recv_sem=rs,
            device_id=(s, me_d), device_id_type=pl.DeviceIdType.MESH,
        )

    def to_dst(d, src, dst, ss, rs):
        return pltpu.make_async_remote_copy(
            src_ref=src, dst_ref=dst, send_sem=ss, recv_sem=rs,
            device_id=(me_s, d), device_id_type=pl.DeviceIdType.MESH,
        )

    def feat(k, d):
        return to_dst(d, x_ref, xs.at[rows(me_d)], xss.at[k], xrs.at[k])

    def part(k, s):
        return to_src(s, bsend.at[k], brecv.at[k], bss.at[k], brs.at[k])

    def back(k, s):
        return to_src(s, gall.at[rows(me_s)], gall.at[rows(me_s)], gss.at[k], grs.at[k])

    def wred(k, s):
        return to_src(s, wsend.at[s], wrecv.at[me_s], wss.at[k], wrs.at[k])

    def fin(k, d):
        return to_dst(d, fsend.at[k], frecv.at[k], fss.at[k], frs.at[k])

    def wdst(k, d):
        return to_dst(d, drecv.at[me_d], drecv.at[me_d], dss.at[k], drs.at[k])

    def wall(k, s):
        return to_src(s, wfin.at[me_s], wfin.at[me_s], ass.at[k], ars.at[k])

    barrier = pltpu.get_barrier_semaphore()

    def greet_src(k, s):
        pl.semaphore_signal(barrier, inc=1, device_id=(s, me_d), device_id_type=pl.DeviceIdType.MESH)

    def greet_dst(k, d):
        pl.semaphore_signal(barrier, inc=1, device_id=(me_s, d), device_id_type=pl.DeviceIdType.MESH)

    src_peers(greet_src)
    dst_peers(greet_dst)
    pl.semaphore_wait(barrier, n_src + n_dst - 2)

    dst_peers(lambda k, d: feat(k, d).start())
    xs[rows(me_d), :] = x_ref[...]

    group = math.gcd(slots, 8)
    turns = slots // group
    eb = group * edges
    lane = lax.broadcasted_iota(jnp.int32, (1, edges), 1)

    def build(turn):
        tgt, src, wgt = [], [], []
        for j in range(group):
            t = turn * group + j
            tid = tid_ref[0, 0, t]
            cnt = cnt_ref[0, 0, t]
            p = pos_ref[0, 0, pl.ds(t, 1), :]
            live = lane < cnt
            row = lax.shift_right_logical(p, 7) + lax.div(tid, n_dst) * TILE
            tgt.append(jnp.where(live, row, -1))
            src.append((p & 127) + lax.rem(tid, n_dst) * TILE)
            if turns == 1:
                wgt.append(ew_ref[0, 0].astype(F32)[j : j + 1, :])
            else:
                at = pl.ds(pl.multiple_of(turn * group, group), group)
                wgt.append(ew_ref[0, 0, at, :].astype(F32)[j : j + 1, :])
        tgt = jnp.concatenate(tgt, axis=1)
        src = jnp.concatenate(src, axis=1)
        wgt = jnp.concatenate(wgt, axis=1)
        spot = lax.broadcasted_iota(jnp.int32, (TILE, eb), 0)

        def col_hot(c):
            ct[rows(c), :] = jnp.where(spot + c * TILE == src, 1.0, 0.0).astype(BF16)

        def row_hot(r):
            rt[rows(r), :] = jnp.where(spot + r * TILE == tgt, wgt, 0.0).astype(BF16)

        def fill(r):
            v = lax.dot_general(rt[rows(r), :], ct[...], NT, preferred_element_type=F32).astype(BF16)
            adj[rows(r), :] = v if turns == 1 else adj[rows(r), :] + v

        def fill_t(c):
            v = lax.dot_general(ct[rows(c), :], rt[...], NT, preferred_element_type=F32).astype(BF16)
            adjt[rows(c), :] = v if turns == 1 else adjt[rows(c), :] + v

        for n, f in ((n_dst, col_hot), (n_src, row_hot), (n_src, fill), (n_dst, fill_t)):
            if n <= 8:
                for i in range(n):
                    f(i)
            else:
                pl.loop(0, n)(f)

    if turns == 1:
        build(0)
    else:
        adj[...] = jnp.zeros_like(adj)
        adjt[...] = jnp.zeros_like(adjt)
        pl.loop(0, turns)(build)

    dst_peers(lambda k, d: feat(k, d).wait_recv())

    def send_part(k, s):
        bsend[k] = jnp.dot(adj[rows(s), :], xs[...], preferred_element_type=F32).astype(BF16)
        part(k, s).start()

    src_peers(send_part)
    agg = jnp.dot(adj[rows(me_s), :], xs[...], preferred_element_type=F32)
    if n_src <= 8:
        for k in range(n_src - 1, 0, -1):
            part(k, flip(me_s, k)).wait_recv()
            agg = agg + brecv[k].astype(F32)
    else:

        def take(k, a):
            part(k, lax.rem(me_s + k, n_src)).wait_recv()
            return a + brecv[k].astype(F32)

        agg = lax.fori_loop(1, n_src, take, agg)
    agg = agg.astype(BF16)

    preact = jnp.dot(agg, w_ref[...], preferred_element_type=F32) + b_ref[...]
    sig = jax.nn.sigmoid(preact)
    gp = (go_ref[...].astype(F32) * sig * (1.0 + preact * (1.0 - sig))).astype(BF16)
    gall[rows(me_s), :] = lax.dot_general(gp, w_ref[...], NT, preferred_element_type=F32).astype(BF16)
    src_peers(lambda k, s: back(k, s).start())
    hid_ref[...] = (preact * sig).astype(BF16)

    dw = jnp.dot(agg.astype(F32).T.astype(BF16), gp, preferred_element_type=F32)
    bs = jnp.sum(gp.astype(F32), axis=0, keepdims=True)
    sub = lax.broadcasted_iota(jnp.int32, (8, 128), 0)
    bv = jnp.where(sub == 0, bs[:, :128], jnp.where(sub == 1, bs[:, 128:], 0.0))
    for q in range(UNITS):
        i, h = q // 2, q % 2
        wsend[q // per, q % per] = dw[8 * i : 8 * i + 8, 128 * h : 128 * h + 128]
    for s in range(n_src):
        wsend[s, per] = bv
    wrecv[me_s] = wsend[me_s]
    src_peers(lambda k, s: wred(k, s).start())

    src_peers(lambda k, s: back(k, s).wait_recv())

    def send_fin(k, d):
        fsend[k] = jnp.dot(adjt[rows(d), :], gall[...], preferred_element_type=F32).astype(BF16)
        fin(k, d).start()

    dst_peers(send_fin)
    own = jnp.dot(adjt[rows(me_d), :], gall[...], preferred_element_type=F32)

    src_peers(lambda k, s: wred(k, s).wait_recv())
    total = wrecv[0]
    for s in range(1, n_src):
        total = total + wrecv[s]
    drecv[me_d] = total
    dst_peers(lambda k, d: wdst(k, d).start())

    dst_peers(lambda k, d: fin(k, d).wait_recv())
    for k in range(1, n_dst):
        own = own + frecv[k].astype(F32)
    ig_ref[...] = own.astype(BF16)

    dst_peers(lambda k, d: wdst(k, d).wait_recv())
    total = drecv[0]
    for d in range(1, n_dst):
        total = total + drecv[d]
    scale = 1.0 / math.sqrt(TILE * n_src * n_dst)
    total = total * scale
    wfin[me_s] = total[:per]
    src_peers(lambda k, s: wall(k, s).start())
    bg_ref[:, :128] = total[per, 0:1, :]
    bg_ref[:, 128:] = total[per, 1:2, :]
    src_peers(lambda k, s: wall(k, s).wait_recv())
    for q in range(UNITS):
        i, h = q // 2, q % 2
        wg_ref[8 * i : 8 * i + 8, 128 * h : 128 * h + 128] = wfin[q // per, q % per]

    for n, copies in ((0, (feat, fin, wdst)), (1, (part, back, wred, wall))):
        for c in copies:
            (src_peers if n else dst_peers)(lambda k, p, c=c: c(k, p).wait_send())


def body(n_src, n_dst, features, weight, bias, tile_index, edge_count, edge_pos, edge_weight, grad_out):
    slots, edges = edge_pos.shape[2], edge_pos.shape[3]
    own = features.shape[0]
    eb = math.gcd(slots, 8) * edges
    per = UNITS // n_src
    vm = pl.BlockSpec(memory_space=pltpu.VMEM)
    sm = pl.BlockSpec(memory_space=pltpu.SMEM)
    dma = pltpu.SemaphoreType.DMA
    s_sems = [dma((n_src,)), dma((n_src,))]
    d_sems = [dma((n_dst,)), dma((n_dst,))]
    hidden, input_grad, weight_grad, bias_grad = pl.pallas_call(
        functools.partial(kernel, n_src, n_dst, slots, edges),
        out_shape=(
            jax.ShapeDtypeStruct((own, F_HID), BF16),
            jax.ShapeDtypeStruct((own, F_IN), BF16),
            jax.ShapeDtypeStruct((F_IN, F_HID), F32),
            jax.ShapeDtypeStruct((1, F_HID), F32),
        ),
        in_specs=[sm, sm, vm, vm, vm, vm, vm, vm],
        out_specs=(vm, vm, vm, vm),
        scratch_shapes=[
            pltpu.VMEM((n_dst * TILE, F_IN), BF16),
            pltpu.VMEM((n_src * TILE, eb), BF16),
            pltpu.VMEM((n_dst * TILE, eb), BF16),
            pltpu.VMEM((n_src * TILE, n_dst * TILE), BF16),
            pltpu.VMEM((n_dst * TILE, n_src * TILE), BF16),
            pltpu.VMEM((n_src, TILE, F_IN), BF16),
            pltpu.VMEM((n_src, TILE, F_IN), BF16),
            pltpu.VMEM((n_src * TILE, F_IN), BF16),
            pltpu.VMEM((n_dst, TILE, F_IN), BF16),
            pltpu.VMEM((n_dst, TILE, F_IN), BF16),
            pltpu.VMEM((n_src, per + 1, 8, 128), F32),
            pltpu.VMEM((n_src, per + 1, 8, 128), F32),
            pltpu.VMEM((n_dst, per + 1, 8, 128), F32),
            pltpu.VMEM((n_src, per, 8, 128), F32),
            *d_sems, *s_sems, *s_sems, *d_sems, *s_sems, *d_sems, *s_sems,
        ],
        compiler_params=pltpu.CompilerParams(
            collective_id=0, has_side_effects=True,
            vmem_limit_bytes=(24 if slots <= 8 else 60) << 20,
        ),
    )(tile_index, edge_count, features, weight, bias.reshape(1, -1), edge_pos, edge_weight, grad_out)
    return hidden, input_grad, weight_grad, bias_grad.reshape(-1)


def solution(mesh):
    placed = (
        P(("src", "dst"), None),
        P(),
        P(),
        P("src", "dst", None),
        P("src", "dst", None),
        P("src", "dst", None, None),
        P("src", "dst", None, None),
        P(("src", "dst"), None),
    )
    return jax.shard_map(
        functools.partial(body, mesh.shape["src"], mesh.shape["dst"]),
        mesh=mesh,
        in_specs=placed,
        out_specs=(P(("src", "dst"), None), P(("src", "dst"), None), P(), P()),
        check_vma=False,
    )
```

```python
import functools
import math

import jax
import jax.numpy as jnp
from jax import lax
from jax.experimental import pallas as pl
from jax.experimental.pallas import tpu as pltpu
from jax.sharding import PartitionSpec as P

TILE = 128
F_IN = 128
F_HID = 256
UNITS = 32
NT = (((1,), (1,)), ((), ()))
F32 = jnp.float32
BF16 = jnp.bfloat16


def flip(me, k):
    out = me
    bit = 1
    while bit <= k:
        if k & bit:
            out = out + bit * (1 - 2 * (lax.div(me, bit) % 2))
        bit *= 2
    return out


def each_peer(n, me, body):
    if n <= 8:
        for k in range(n - 1, 0, -1):
            body(k, flip(me, k))
    else:

        def step(k, carry):
            body(k, lax.rem(me + k, n))
            return carry

        lax.fori_loop(1, n, step, 0)


def rows(i, n=TILE):
    return pl.ds(pl.multiple_of(i * n, n), n)


def kernel(
    n_src, n_dst, slots, edges,
    tid_ref, cnt_ref, x_hbm, w_hbm, b_hbm, pos_hbm, ew_hbm, go_hbm,
    hid_out, ig_out, wg_out, bg_out,
    hid_ref, ig_ref, wg_ref, bg_ref, outs,
    x_ref, w_ref, b_ref, pos_ref, ew_ref, go_ref,
    xs, rt, ct, adj, adjt, bsend, brecv, gall, fsend, frecv,
    wsend, drecv, ssend, srecv, wcol, wfin,
    ins, xss, xrs, bss, brs, gss, grs, fss, frs, dss, drs, wss, wrs, css, crs, ass, ars,
):
    me_s = lax.axis_index("src")
    me_d = lax.axis_index("dst")
    relay = n_src == 8
    ud = UNITS // n_dst
    pu = ud // n_src
    src_peers = functools.partial(each_peer, n_src, me_s)
    dst_peers = functools.partial(each_peer, n_dst, me_d)

    def to_src(s, src, dst, ss, rs):
        return pltpu.make_async_remote_copy(
            src_ref=src, dst_ref=dst, send_sem=ss, recv_sem=rs,
            device_id=(s, me_d), device_id_type=pl.DeviceIdType.MESH,
        )

    def to_dst(d, src, dst, ss, rs):
        return pltpu.make_async_remote_copy(
            src_ref=src, dst_ref=dst, send_sem=ss, recv_sem=rs,
            device_id=(me_s, d), device_id_type=pl.DeviceIdType.MESH,
        )

    def feat(k, d):
        return to_dst(d, x_ref, xs.at[rows(me_d)], xss.at[k], xrs.at[k])

    def part(k, s):
        if relay and k in (5, 7):
            s = flip(me_s, 1)
        return to_src(s, bsend.at[k], brecv.at[k], bss.at[k], brs.at[k])

    def back(k, s):
        block = me_s
        if relay and k in (5, 7):
            s, block = flip(me_s, 1), flip(me_s, k - 1)
        return to_src(s, gall.at[rows(block)], gall.at[rows(block)], gss.at[k], grs.at[k])

    def fin(k, d):
        return to_dst(d, fsend.at[k], frecv.at[k], fss.at[k], frs.at[k])

    def wdst(k, d):
        return to_dst(d, wsend.at[d], drecv.at[me_d], dss.at[k], drs.at[k])

    def wsrc(k, s):
        return to_src(s, ssend.at[s if pu else 0], srecv.at[me_s], wss.at[k], wrs.at[k])

    def wcolumn(k, s):
        return to_src(s, wcol.at[me_s], wcol.at[me_s], css.at[k], crs.at[k])

    def wall(k, d):
        return to_dst(d, wfin.at[me_d], wfin.at[me_d], ass.at[k], ars.at[k])

    loads = [
        pltpu.make_async_copy(a, b, ins.at[i])
        for i, (a, b) in enumerate((
            (x_hbm, x_ref), (pos_hbm, pos_ref), (ew_hbm, ew_ref),
            (w_hbm, w_ref), (b_hbm, b_ref), (go_hbm, go_ref),
        ))
    ]
    for c in loads:
        c.start()
    stores = [
        pltpu.make_async_copy(a, b, outs.at[i])
        for i, (a, b) in enumerate((
            (hid_ref, hid_out), (ig_ref, ig_out), (wg_ref, wg_out), (bg_ref, bg_out),
        ))
    ]

    barrier = pltpu.get_barrier_semaphore()

    def greet_src(k, s):
        pl.semaphore_signal(barrier, inc=1, device_id=(s, me_d), device_id_type=pl.DeviceIdType.MESH)

    def greet_dst(k, d):
        pl.semaphore_signal(barrier, inc=1, device_id=(me_s, d), device_id_type=pl.DeviceIdType.MESH)

    src_peers(greet_src)
    dst_peers(greet_dst)
    pl.semaphore_wait(barrier, n_src + n_dst - 2)

    loads[0].wait()
    dst_peers(lambda k, d: feat(k, d).start())
    xs[rows(me_d), :] = x_ref[...]

    loads[1].wait()
    loads[2].wait()

    group = math.gcd(slots, 16)
    turns = slots // group
    eb = group * edges
    lane = lax.broadcasted_iota(jnp.int32, (1, edges), 1)

    def build(turn):
        tgt, src, wgt = [], [], []
        for j in range(group):
            t = turn * group + j
            tid = tid_ref[0, 0, t]
            cnt = cnt_ref[0, 0, t]
            p = pos_ref[0, 0, pl.ds(t, 1), :]
            live = lane < cnt
            row = lax.shift_right_logical(p, 7) + lax.div(tid, n_dst) * TILE
            tgt.append(jnp.where(live, row, -1))
            src.append((p & 127) + lax.rem(tid, n_dst) * TILE)
            if turns == 1:
                wgt.append(ew_ref[0, 0].astype(F32)[j : j + 1, :])
            else:
                at = pl.ds(pl.multiple_of(turn * group, group), group)
                wgt.append(ew_ref[0, 0, at, :].astype(F32)[j : j + 1, :])
        tgt = jnp.concatenate(tgt, axis=1)
        src = jnp.concatenate(src, axis=1)
        wgt = jnp.concatenate(wgt, axis=1)
        spot = lax.broadcasted_iota(jnp.int32, (TILE, eb), 0)

        def col_hot(c):
            ct[rows(c), :] = jnp.where(spot + c * TILE == src, 1.0, 0.0).astype(BF16)

        def row_hot(r):
            rt[rows(r), :] = jnp.where(spot + r * TILE == tgt, wgt, 0.0).astype(BF16)

        def fill(r):
            v = lax.dot_general(rt[rows(r), :], ct[...], NT, preferred_element_type=F32).astype(BF16)
            adj[rows(r), :] = v if turns == 1 else adj[rows(r), :] + v

        def fill_t(c):
            v = lax.dot_general(ct[rows(c), :], rt[...], NT, preferred_element_type=F32).astype(BF16)
            adjt[rows(c), :] = v if turns == 1 else adjt[rows(c), :] + v

        for n, f in ((n_dst, col_hot), (n_src, row_hot), (n_src, fill), (n_dst, fill_t)):
            if n <= 8:
                for i in range(n):
                    f(i)
            else:
                pl.loop(0, n)(f)

    if turns == 1:
        build(0)
    else:
        adj[...] = jnp.zeros_like(adj)
        adjt[...] = jnp.zeros_like(adjt)
        pl.loop(0, turns)(build)

    dst_peers(lambda k, d: feat(k, d).wait_recv())

    def partial_rows(s):
        return jnp.dot(adj[rows(s), :], xs[...], preferred_element_type=F32)

    def send_part(k, s):
        bsend[k] = partial_rows(s).astype(BF16)
        part(k, s).start()

    if relay:
        for k in (7, 5, 3, 2, 1):
            send_part(k, flip(me_s, k))
        for k in (6, 4):
            far = partial_rows(flip(me_s, k))
            part(k + 1, me_s).wait_recv()
            bsend[k] = (far + brecv[k + 1].astype(F32)).astype(BF16)
            part(k, flip(me_s, k)).start()
    else:
        src_peers(send_part)
    agg = partial_rows(me_s)
    for c in loads[3:]:
        c.wait()
    if relay:
        for k in (1, 2, 3, 6, 4):
            part(k, flip(me_s, k)).wait_recv()
            agg = agg + brecv[k].astype(F32)
    else:

        def take(k, a):
            part(k, lax.rem(me_s + k, n_src)).wait_recv()
            return a + brecv[k].astype(F32)

        agg = lax.fori_loop(1, n_src, take, agg)
    agg = agg.astype(BF16)

    preact = jnp.dot(agg, w_ref[...], preferred_element_type=F32) + b_ref[...]
    sig = jax.nn.sigmoid(preact)
    gp = (go_ref[...].astype(F32) * sig * (1.0 + preact * (1.0 - sig))).astype(BF16)
    gall[rows(me_s), :] = lax.dot_general(gp, w_ref[...], NT, preferred_element_type=F32).astype(BF16)
    if relay:
        for k in (6, 4, 1, 2, 3):
            back(k, flip(me_s, k)).start()
    else:
        src_peers(lambda k, s: back(k, s).start())
    hid_ref[...] = (preact * sig).astype(BF16)
    stores[0].start()

    dw = jnp.dot(agg.astype(F32).T.astype(BF16), gp, preferred_element_type=F32)
    bs = jnp.sum(gp.astype(F32), axis=0, keepdims=True)
    sub = lax.broadcasted_iota(jnp.int32, (8, 128), 0)
    bv = jnp.where(sub == 0, bs[:, :128], jnp.where(sub == 1, bs[:, 128:], 0.0))
    for q in range(UNITS):
        i, h = q // 2, q % 2
        wsend[q // ud, q % ud] = dw[8 * i : 8 * i + 8, 128 * h : 128 * h + 128]
    for d in range(n_dst):
        wsend[d, ud] = bv
    drecv[me_d] = wsend[me_d]
    dst_peers(lambda k, d: wdst(k, d).start())

    if relay:
        for k in (6, 4):
            back(k, flip(me_s, k)).wait_recv()
            back(k + 1, me_s).start()

    def ordered(ref, n):
        total = ref[0]
        for i in range(1, n):
            total = total + ref[i]
        return total

    scale = 1.0 / math.sqrt(TILE * n_src * n_dst)
    dst_peers(lambda k, d: wdst(k, d).wait_recv())
    chunk = ordered(drecv, n_dst)
    if pu:
        for s in range(n_src):
            ssend[s, :pu] = chunk[s * pu : s * pu + pu]
            ssend[s, pu] = chunk[ud]
        srecv[me_s] = ssend[me_s]
    else:
        ssend[0] = chunk
        srecv[me_s] = chunk
    src_peers(lambda k, s: wsrc(k, s).start())
    src_peers(lambda k, s: wsrc(k, s).wait_recv())
    total = ordered(srecv, n_src) * scale
    if pu:
        wcol[me_s] = total[:pu]
        src_peers(lambda k, s: wcolumn(k, s).start())

    if relay:
        for k in (1, 2, 3, 7, 5):
            back(k, flip(me_s, k)).wait_recv()
    else:
        src_peers(lambda k, s: back(k, s).wait_recv())

    def send_fin(k, d):
        fsend[k] = jnp.dot(adjt[rows(d), :], gall[...], preferred_element_type=F32).astype(BF16)
        fin(k, d).start()

    dst_peers(send_fin)
    own = jnp.dot(adjt[rows(me_d), :], gall[...], preferred_element_type=F32)

    if pu:
        src_peers(lambda k, s: wcolumn(k, s).wait_recv())
        wfin[me_d] = wcol[...].reshape(ud * 8, 128).astype(BF16)
    else:
        wfin[me_d] = total[:ud].reshape(ud * 8, 128).astype(BF16)
    dst_peers(lambda k, d: wall(k, d).start())
    last = -1
    bg_ref[:, :128] = total[last, 0:1, :]
    bg_ref[:, 128:] = total[last, 1:2, :]
    stores[3].start()

    for k in range(n_dst - 1, 0, -1):
        fin(k, me_d).wait_recv()
        own = own + frecv[k].astype(F32)
    ig_ref[...] = own.astype(BF16)
    stores[1].start()

    dst_peers(lambda k, d: wall(k, d).wait_recv())
    for q in range(UNITS):
        i, h = q // 2, q % 2
        at = 8 * (q % ud)
        wg_ref[8 * i : 8 * i + 8, 128 * h : 128 * h + 128] = wfin[q // ud, at : at + 8, :].astype(F32)
    stores[2].start()

    src_copies = (part, back, wsrc, wcolumn) if pu else (part, back, wsrc)
    for c in (feat, fin, wdst, wall):
        dst_peers(lambda k, p, c=c: c(k, p).wait_send())
    for c in src_copies:
        src_peers(lambda k, p, c=c: c(k, p).wait_send())
    for c in stores:
        c.wait()


def store(h_in, i_in, w_in, b_in, h_out, i_out, w_out, b_out, sems):
    pairs = ((h_in, h_out), (i_in, i_out), (w_in, w_out), (b_in, b_out))
    copies = [pltpu.make_async_copy(a, b, sems.at[i]) for i, (a, b) in enumerate(pairs)]
    for c in copies:
        c.start()
    for c in copies:
        c.wait()


def body(n_src, n_dst, features, weight, bias, tile_index, edge_count, edge_pos, edge_weight, grad_out):
    slots, edges = edge_pos.shape[2], edge_pos.shape[3]
    own = features.shape[0]
    eb = math.gcd(slots, 16) * edges
    ud = UNITS // n_dst
    pu = ud // n_src
    sm = pl.BlockSpec(memory_space=pltpu.SMEM)
    hbm = pl.BlockSpec(memory_space=pltpu.HBM)
    anyw = pl.BlockSpec(memory_space=pl.ANY)
    dma = pltpu.SemaphoreType.DMA
    s_sems = [dma((n_src,)), dma((n_src,))]
    d_sems = [dma((n_dst,)), dma((n_dst,))]
    outs = (
        jax.ShapeDtypeStruct((own, F_HID), BF16),
        jax.ShapeDtypeStruct((own, F_IN), BF16),
        jax.ShapeDtypeStruct((F_IN, F_HID), F32),
        jax.ShapeDtypeStruct((1, F_HID), F32),
    )
    arrays = (features, weight, bias.reshape(1, -1), edge_pos, edge_weight, grad_out)
    piece = (pu or ud) + 1
    results = pl.pallas_call(
        functools.partial(kernel, n_src, n_dst, slots, edges),
        out_shape=outs,
        in_specs=[sm, sm, *[hbm] * 6],
        out_specs=(anyw,) * 4,
        scratch_shapes=[
            *[pltpu.VMEM(a.shape, a.dtype) for a in outs],
            dma((4,)),
            *[pltpu.VMEM(a.shape, a.dtype) for a in arrays],
            pltpu.VMEM((n_dst * TILE, F_IN), BF16),
            pltpu.VMEM((n_src * TILE, eb), BF16),
            pltpu.VMEM((n_dst * TILE, eb), BF16),
            pltpu.VMEM((n_src * TILE, n_dst * TILE), BF16),
            pltpu.VMEM((n_dst * TILE, n_src * TILE), BF16),
            pltpu.VMEM((n_src, TILE, F_IN), BF16),
            pltpu.VMEM((n_src, TILE, F_IN), BF16),
            pltpu.VMEM((n_src * TILE, F_IN), BF16),
            pltpu.VMEM((n_dst, TILE, F_IN), BF16),
            pltpu.VMEM((n_dst, TILE, F_IN), BF16),
            pltpu.VMEM((n_dst, ud + 1, 8, 128), F32),
            pltpu.VMEM((n_dst, ud + 1, 8, 128), F32),
            pltpu.VMEM((n_src if pu else 1, piece, 8, 128), F32),
            pltpu.VMEM((n_src, piece, 8, 128), F32),
            pltpu.VMEM((n_src, max(pu, 1), 8, 128), F32),
            pltpu.VMEM((n_dst, ud * 8, 128), BF16),
            dma((len(arrays),)),
            *d_sems, *s_sems, *s_sems, *d_sems, *d_sems, *s_sems, *s_sems, *d_sems,
        ],
        compiler_params=pltpu.CompilerParams(
            collective_id=0, has_side_effects=True,
            vmem_limit_bytes=64 << 20,
        ),
    )(tile_index, edge_count, *arrays)
    hidden, input_grad, weight_grad, bias_grad = pl.pallas_call(
        store,
        out_shape=outs,
        in_specs=[anyw] * 4,
        out_specs=(anyw,) * 4,
        scratch_shapes=[dma((4,))],
        compiler_params=pltpu.CompilerParams(vmem_limit_bytes=64 << 20),
    )(*results)
    return hidden, input_grad, weight_grad, bias_grad.reshape(-1)


def solution(mesh):
    placed = (
        P(("src", "dst"), None),
        P(),
        P(),
        P("src", "dst", None),
        P("src", "dst", None),
        P("src", "dst", None, None),
        P("src", "dst", None, None),
        P(("src", "dst"), None),
    )
    return jax.shard_map(
        functools.partial(body, mesh.shape["src"], mesh.shape["dst"]),
        mesh=mesh,
        in_specs=placed,
        out_specs=(P(("src", "dst"), None), P(("src", "dst"), None), P(), P()),
        check_vma=False,
    )
```

```python
import functools
import math

import jax
import jax.numpy as jnp
from jax import lax
from jax.experimental import pallas as pl
from jax.experimental.pallas import tpu as pltpu
from jax.sharding import PartitionSpec as P

TILE = 128
F_IN = 128
F_HID = 256
UNITS = 32
F32 = jnp.float32
BF16 = jnp.bfloat16


def flip(me, k):
    out = me
    bit = 1
    while bit <= k:
        if k & bit:
            out = out + bit * (1 - 2 * (lax.div(me, bit) % 2))
        bit *= 2
    return out


def each_peer(n, me, body):
    if n <= 8:
        for k in range(n - 1, 0, -1):
            body(k, flip(me, k))
    else:

        def step(k, carry):
            body(k, lax.rem(me + k, n))
            return carry

        lax.fori_loop(1, n, step, 0)


def rows(i, n=TILE):
    return pl.ds(pl.multiple_of(i * n, n), n)


def kernel(
    n_src, n_dst, slots, edges,
    tid_ref, cnt_ref, x_hbm, w_hbm, b_hbm, pos_hbm, ew_hbm, go_hbm,
    hid_ref, ig_ref, wg_ref, bg_ref,
    x_ref, w_ref, b_ref, pos_ref, ew_ref, go_ref,
    xs, rt, ct, hot_s, hot_t, picked, facc, bacc, wt, bsend, brecv, gall, fsend, frecv,
    wsend, drecv, ssend, srecv, wcol, wfin,
    ins, xss, xrs, bss, brs, gss, grs, fss, frs, dss, drs, wss, wrs, css, crs, ass, ars,
):
    me_s = lax.axis_index("src")
    me_d = lax.axis_index("dst")
    relay = n_src == 8
    ud = UNITS // n_dst
    pu = ud // n_src
    src_peers = functools.partial(each_peer, n_src, me_s)
    dst_peers = functools.partial(each_peer, n_dst, me_d)

    def to_src(s, src, dst, ss, rs):
        return pltpu.make_async_remote_copy(
            src_ref=src, dst_ref=dst, send_sem=ss, recv_sem=rs,
            device_id=(s, me_d), device_id_type=pl.DeviceIdType.MESH,
        )

    def to_dst(d, src, dst, ss, rs):
        return pltpu.make_async_remote_copy(
            src_ref=src, dst_ref=dst, send_sem=ss, recv_sem=rs,
            device_id=(me_s, d), device_id_type=pl.DeviceIdType.MESH,
        )

    def feat(k, d):
        return to_dst(d, x_ref, xs.at[me_d], xss.at[k], xrs.at[k])

    def part(k, s):
        if relay and k in (5, 7):
            s = flip(me_s, 1)
        return to_src(s, bsend.at[k], brecv.at[k], bss.at[k], brs.at[k])

    def back(k, s):
        block = me_s
        if relay and k in (5, 7):
            s, block = flip(me_s, 1), flip(me_s, k - 1)
        return to_src(s, gall.at[block], gall.at[block], gss.at[k], grs.at[k])

    def fin(k, d):
        return to_dst(d, fsend.at[k], frecv.at[k], fss.at[k], frs.at[k])

    def wdst(k, d):
        return to_dst(d, wsend.at[d], drecv.at[me_d], dss.at[k], drs.at[k])

    def wsrc(k, s):
        return to_src(s, ssend.at[s if pu else 0], srecv.at[me_s], wss.at[k], wrs.at[k])

    def wcolumn(k, s):
        return to_src(s, wcol.at[me_s], wcol.at[me_s], css.at[k], crs.at[k])

    def wall(k, d):
        return to_dst(d, wfin.at[me_d], wfin.at[me_d], ass.at[k], ars.at[k])

    loads = [
        pltpu.make_async_copy(a, b, ins.at[i])
        for i, (a, b) in enumerate((
            (x_hbm, x_ref), (pos_hbm, pos_ref), (ew_hbm, ew_ref),
            (w_hbm, w_ref), (b_hbm, b_ref), (go_hbm, go_ref),
        ))
    ]
    for c in loads:
        c.start()

    barrier = pltpu.get_barrier_semaphore()

    def greet_src(k, s):
        pl.semaphore_signal(barrier, inc=1, device_id=(s, me_d), device_id_type=pl.DeviceIdType.MESH)

    def greet_dst(k, d):
        pl.semaphore_signal(barrier, inc=1, device_id=(me_s, d), device_id_type=pl.DeviceIdType.MESH)

    src_peers(greet_src)
    dst_peers(greet_dst)
    pl.semaphore_wait(barrier, n_src + n_dst - 2)

    loads[0].wait()
    dst_peers(lambda k, d: feat(k, d).start())
    xs[me_d] = x_ref[...]

    loads[1].wait()
    loads[2].wait()

    group = math.gcd(slots, 16)
    turns = slots // group
    eb = group * edges
    lane = lax.broadcasted_iota(jnp.int32, (1, edges), 1)

    def group_slots(turn):
        if turns == 1:
            return slice(None)
        return pl.ds(pl.multiple_of(turn * group, group), group)

    def build(turn):
        at = group_slots(turn)
        pos = pos_ref[0, 0, at, :]
        weights = ew_ref[0, 0, at, :].astype(F32)
        across = lax.broadcasted_iota(jnp.int32, (edges, TILE), 1)
        turned = pos.T
        tgt, src, wgt = [], [], []
        for j in range(group):
            t = turn * group + j
            tid = tid_ref[0, 0, t]
            p = pos[j : j + 1, :]
            tgt.append(lax.shift_right_logical(p, 7) + lax.div(tid, n_dst) * TILE)
            src.append((p & 127) + lax.rem(tid, n_dst) * TILE)
            wgt.append(jnp.where(lane < cnt_ref[0, 0, t], weights[j : j + 1, :], 0.0))
            c = turned[:, j : j + 1]
            hot_s[j] = jnp.where((c & 127) == across, 1.0, 0.0).astype(BF16)
            hot_t[j] = jnp.where(lax.shift_right_logical(c, 7) == across, 1.0, 0.0).astype(BF16)
        tgt = jnp.concatenate(tgt, axis=1)
        src = jnp.concatenate(src, axis=1)
        wgt = jnp.concatenate(wgt, axis=1)
        spot = lax.broadcasted_iota(jnp.int32, (TILE, eb), 0)

        def col_hot(c):
            ct[rows(c), :] = jnp.where(spot == src - c * TILE, wgt, 0.0).astype(BF16)

        def row_hot(r):
            rt[rows(r), :] = jnp.where(spot == tgt - r * TILE, wgt, 0.0).astype(BF16)

        for n, f in ((n_src, row_hot), (n_dst, col_hot)):
            if n <= 8:
                for i in range(n):
                    f(i)
            else:
                pl.loop(0, n)(f)

    def gather(turn, hot, table, tile_of):
        for j in range(group):
            i = tile_of(tid_ref[0, 0, turn * group + j])
            block = table[i]
            picked[j * edges : (j + 1) * edges, :] = jnp.dot(
                hot[j], block, preferred_element_type=F32
            ).astype(BF16)

    def spread(hot, i):
        return jnp.dot(hot[rows(i), :], picked[...], preferred_element_type=F32)

    def all_turns(hot, table, tile_of, scatter, acc, n):
        acc[...] = jnp.zeros_like(acc)

        @pl.loop(0, turns)
        def _(turn):
            build(turn)
            gather(turn, hot, table, tile_of)

            @pl.loop(0, n)
            def _(i):
                acc[i] += spread(scatter, i)

    if turns == 1:
        build(0)
    for c in loads[3:]:
        c.wait()
    wt[...] = w_ref[...].astype(F32).T.astype(BF16)
    dst_peers(lambda k, d: feat(k, d).wait_recv())
    if turns == 1:
        gather(0, hot_s, xs, lambda tid: lax.rem(tid, n_dst))
    else:
        all_turns(hot_s, xs, lambda tid: lax.rem(tid, n_dst), rt, facc, n_src)

    def partial_rows(s):
        return spread(rt, s) if turns == 1 else facc[s]

    def send_part(k, s):
        bsend[k] = partial_rows(s).astype(BF16)
        part(k, s).start()

    if relay:
        for k in (7, 5, 3, 2, 1):
            send_part(k, flip(me_s, k))
        for k in (6, 4):
            far = partial_rows(flip(me_s, k))
            part(k + 1, me_s).wait_recv()
            bsend[k] = (far + brecv[k + 1].astype(F32)).astype(BF16)
            part(k, flip(me_s, k)).start()
    else:
        src_peers(send_part)
    agg = partial_rows(me_s)
    if relay:
        for k in (1, 2, 3, 6, 4):
            part(k, flip(me_s, k)).wait_recv()
            agg = agg + brecv[k].astype(F32)
    else:

        def take(k, a):
            part(k, lax.rem(me_s + k, n_src)).wait_recv()
            return a + brecv[k].astype(F32)

        agg = lax.fori_loop(1, n_src, take, agg)
    agg = agg.astype(BF16)

    preact = jnp.dot(agg, w_ref[...], preferred_element_type=F32) + b_ref[...]
    sig = jax.nn.sigmoid(preact)
    gp = (go_ref[...].astype(F32) * sig * (1.0 + preact * (1.0 - sig))).astype(BF16)
    gall[me_s] = jnp.dot(gp, wt[...], preferred_element_type=F32).astype(BF16)
    if relay:
        for k in (6, 4, 1, 2, 3):
            back(k, flip(me_s, k)).start()
    else:
        src_peers(lambda k, s: back(k, s).start())
    hid_ref[...] = (preact * sig).astype(BF16)

    dw = jnp.dot(agg.astype(F32).T.astype(BF16), gp, preferred_element_type=F32)
    bs = jnp.sum(gp.astype(F32), axis=0, keepdims=True)
    sub = lax.broadcasted_iota(jnp.int32, (8, 128), 0)
    bv = jnp.where(sub == 0, bs[:, :128], jnp.where(sub == 1, bs[:, 128:], 0.0))
    for q in range(UNITS):
        i, h = q // 2, q % 2
        wsend[q // ud, q % ud] = dw[8 * i : 8 * i + 8, 128 * h : 128 * h + 128]
    for d in range(n_dst):
        wsend[d, ud] = bv
    drecv[me_d] = wsend[me_d]
    dst_peers(lambda k, d: wdst(k, d).start())

    if relay:
        for k in (6, 4):
            back(k, flip(me_s, k)).wait_recv()
            back(k + 1, me_s).start()

    def ordered(ref, n):
        total = ref[0]
        for i in range(1, n):
            total = total + ref[i]
        return total

    scale = 1.0 / math.sqrt(TILE * n_src * n_dst)
    dst_peers(lambda k, d: wdst(k, d).wait_recv())
    chunk = ordered(drecv, n_dst)
    if pu:
        for s in range(n_src):
            ssend[s, :pu] = chunk[s * pu : s * pu + pu]
            ssend[s, pu] = chunk[ud]
        srecv[me_s] = ssend[me_s]
    else:
        ssend[0] = chunk
        srecv[me_s] = chunk
    src_peers(lambda k, s: wsrc(k, s).start())
    src_peers(lambda k, s: wsrc(k, s).wait_recv())
    total = ordered(srecv, n_src) * scale
    if pu:
        wcol[me_s] = total[:pu]
        src_peers(lambda k, s: wcolumn(k, s).start())

    if relay:
        for k in (1, 2, 3, 7, 5):
            back(k, flip(me_s, k)).wait_recv()
    else:
        src_peers(lambda k, s: back(k, s).wait_recv())

    if turns == 1:
        gather(0, hot_t, gall, lambda tid: lax.div(tid, n_dst))
    else:
        all_turns(hot_t, gall, lambda tid: lax.div(tid, n_dst), ct, bacc, n_dst)

    def back_rows(d):
        return spread(ct, d) if turns == 1 else bacc[d]

    def send_fin(k, d):
        fsend[k] = back_rows(d).astype(BF16)
        fin(k, d).start()

    dst_peers(send_fin)
    own = back_rows(me_d)

    if pu:
        src_peers(lambda k, s: wcolumn(k, s).wait_recv())
        wfin[me_d] = wcol[...].reshape(ud * 8, 128).astype(BF16)
    else:
        wfin[me_d] = total[:ud].reshape(ud * 8, 128).astype(BF16)
    dst_peers(lambda k, d: wall(k, d).start())
    last = -1
    bg_ref[:, :128] = total[last, 0:1, :]
    bg_ref[:, 128:] = total[last, 1:2, :]

    for k in range(n_dst - 1, 0, -1):
        fin(k, me_d).wait_recv()
        own = own + frecv[k].astype(F32)
    ig_ref[...] = own.astype(BF16)

    dst_peers(lambda k, d: wall(k, d).wait_recv())
    for q in range(UNITS):
        i, h = q // 2, q % 2
        at = 8 * (q % ud)
        wg_ref[8 * i : 8 * i + 8, 128 * h : 128 * h + 128] = wfin[q // ud, at : at + 8, :].astype(F32)

    src_copies = (part, back, wsrc, wcolumn) if pu else (part, back, wsrc)
    for c in (feat, fin, wdst, wall):
        dst_peers(lambda k, p, c=c: c(k, p).wait_send())
    for c in src_copies:
        src_peers(lambda k, p, c=c: c(k, p).wait_send())


def store(h_in, i_in, w_in, b_in, h_out, i_out, w_out, b_out, sems):
    pairs = ((h_in, h_out), (i_in, i_out), (w_in, w_out), (b_in, b_out))
    copies = [pltpu.make_async_copy(a, b, sems.at[i]) for i, (a, b) in enumerate(pairs)]
    for c in copies:
        c.start()
    for c in copies:
        c.wait()


def body(n_src, n_dst, features, weight, bias, tile_index, edge_count, edge_pos, edge_weight, grad_out):
    slots, edges = edge_pos.shape[2], edge_pos.shape[3]
    own = features.shape[0]
    group = math.gcd(slots, 16)
    eb = group * edges
    many = slots > group
    ud = UNITS // n_dst
    pu = ud // n_src
    vm = pl.BlockSpec(memory_space=pltpu.VMEM)
    sm = pl.BlockSpec(memory_space=pltpu.SMEM)
    hbm = pl.BlockSpec(memory_space=pltpu.HBM)
    anyw = pl.BlockSpec(memory_space=pl.ANY)
    dma = pltpu.SemaphoreType.DMA
    s_sems = [dma((n_src,)), dma((n_src,))]
    d_sems = [dma((n_dst,)), dma((n_dst,))]
    outs = (
        jax.ShapeDtypeStruct((own, F_HID), BF16),
        jax.ShapeDtypeStruct((own, F_IN), BF16),
        jax.ShapeDtypeStruct((F_IN, F_HID), F32),
        jax.ShapeDtypeStruct((1, F_HID), F32),
    )
    arrays = (features, weight, bias.reshape(1, -1), edge_pos, edge_weight, grad_out)
    piece = (pu or ud) + 1
    results = pl.pallas_call(
        functools.partial(kernel, n_src, n_dst, slots, edges),
        out_shape=tuple(pltpu.VMEM(o.shape, o.dtype) for o in outs),
        in_specs=[sm, sm, *[hbm] * 6],
        out_specs=(vm,) * 4,
        scratch_shapes=[
            *[pltpu.VMEM(a.shape, a.dtype) for a in arrays],
            pltpu.VMEM((n_dst, TILE, F_IN), BF16),
            pltpu.VMEM((n_src * TILE, eb), BF16),
            pltpu.VMEM((n_dst * TILE, eb), BF16),
            pltpu.VMEM((group, edges, TILE), BF16),
            pltpu.VMEM((group, edges, TILE), BF16),
            pltpu.VMEM((eb, F_IN), BF16),
            pltpu.VMEM((n_src if many else 1, TILE, F_IN), F32),
            pltpu.VMEM((n_dst if many else 1, TILE, F_IN), F32),
            pltpu.VMEM((F_HID, F_IN), BF16),
            pltpu.VMEM((n_src, TILE, F_IN), BF16),
            pltpu.VMEM((n_src, TILE, F_IN), BF16),
            pltpu.VMEM((n_src, TILE, F_IN), BF16),
            pltpu.VMEM((n_dst, TILE, F_IN), BF16),
            pltpu.VMEM((n_dst, TILE, F_IN), BF16),
            pltpu.VMEM((n_dst, ud + 1, 8, 128), F32),
            pltpu.VMEM((n_dst, ud + 1, 8, 128), F32),
            pltpu.VMEM((n_src if pu else 1, piece, 8, 128), F32),
            pltpu.VMEM((n_src, piece, 8, 128), F32),
            pltpu.VMEM((n_src, max(pu, 1), 8, 128), F32),
            pltpu.VMEM((n_dst, ud * 8, 128), BF16),
            dma((len(arrays),)),
            *d_sems, *s_sems, *s_sems, *d_sems, *d_sems, *s_sems, *s_sems, *d_sems,
        ],
        compiler_params=pltpu.CompilerParams(
            collective_id=0, has_side_effects=True,
            vmem_limit_bytes=(64 << 20) - (1024 << 10),
        ),
    )(tile_index, edge_count, *arrays)
    hidden, input_grad, weight_grad, bias_grad = pl.pallas_call(
        store,
        out_shape=outs,
        in_specs=[anyw] * 4,
        out_specs=(anyw,) * 4,
        scratch_shapes=[dma((4,))],
    )(*results)
    return hidden, input_grad, weight_grad, bias_grad.reshape(-1)


def solution(mesh):
    placed = (
        P(("src", "dst"), None),
        P(),
        P(),
        P("src", "dst", None),
        P("src", "dst", None),
        P("src", "dst", None, None),
        P("src", "dst", None, None),
        P(("src", "dst"), None),
    )
    return jax.shard_map(
        functools.partial(body, mesh.shape["src"], mesh.shape["dst"]),
        mesh=mesh,
        in_specs=placed,
        out_specs=(P(("src", "dst"), None), P(("src", "dst"), None), P(), P()),
        check_vma=False,
    )
```

```python
import functools
import math

import jax
import jax.numpy as jnp
from jax import lax
from jax.experimental import pallas as pl
from jax.experimental.pallas import tpu as pltpu
from jax.sharding import PartitionSpec as P

TILE = 128
F_IN = 128
F_HID = 256
UNITS = 32
F32 = jnp.float32
BF16 = jnp.bfloat16


def flip(me, k):
    out = me
    bit = 1
    while bit <= k:
        if k & bit:
            out = out + bit * (1 - 2 * (lax.div(me, bit) % 2))
        bit *= 2
    return out


def each_peer(n, me, body):
    if n <= 8:
        for k in range(n - 1, 0, -1):
            body(k, flip(me, k))
    else:

        def step(k, carry):
            body(k, lax.rem(me + k, n))
            return carry

        lax.fori_loop(1, n, step, 0)


def rows(i, n=TILE):
    return pl.ds(pl.multiple_of(i * n, n), n)


def kernel(
    n_src, n_dst, slots, edges,
    tid_ref, cnt_ref, x_hbm, w_hbm, b_hbm, pos_hbm, ew_hbm, go_hbm,
    hid_ref, ig_ref, wg_ref, bg_ref,
    w_ref, b_ref, pos_ref, ew_ref, go_ref,
    xs, rt, ct, hot_s, hot_t, picked, facc, bacc, wt, bsend, brecv, gall, fsend, frecv,
    wsend, drecv, ssend, srecv, wcol, wfin,
    ins, xss, xrs, bss, brs, gss, grs, fss, frs, dss, drs, wss, wrs, css, crs, ass, ars,
):
    me_s = lax.axis_index("src")
    me_d = lax.axis_index("dst")
    relay = n_src == 8
    ud = UNITS // n_dst
    pu = ud // n_src
    src_peers = functools.partial(each_peer, n_src, me_s)
    dst_peers = functools.partial(each_peer, n_dst, me_d)

    def to_src(s, src, dst, ss, rs):
        return pltpu.make_async_remote_copy(
            src_ref=src, dst_ref=dst, send_sem=ss, recv_sem=rs,
            device_id=(s, me_d), device_id_type=pl.DeviceIdType.MESH,
        )

    def to_dst(d, src, dst, ss, rs):
        return pltpu.make_async_remote_copy(
            src_ref=src, dst_ref=dst, send_sem=ss, recv_sem=rs,
            device_id=(me_s, d), device_id_type=pl.DeviceIdType.MESH,
        )

    def feat(k, d):
        return to_dst(d, x_hbm, xs.at[me_d], xss.at[k], xrs.at[k])

    def part(k, s):
        if relay and k == 5:
            s = flip(me_s, 1)
        return to_src(s, bsend.at[k], brecv.at[k], bss.at[k], brs.at[k])

    def back(k, s):
        block = me_s
        if relay and k == 5:
            s, block = flip(me_s, 1), flip(me_s, 4)
        return to_src(s, gall.at[block], gall.at[block], gss.at[k], grs.at[k])

    def fin(k, d):
        return to_dst(d, fsend.at[k], frecv.at[k], fss.at[k], frs.at[k])

    def wdst(k, d):
        return to_dst(d, wsend.at[d], drecv.at[me_d], dss.at[k], drs.at[k])

    def wsrc(k, s):
        return to_src(s, ssend.at[s if pu else 0], srecv.at[me_s], wss.at[k], wrs.at[k])

    def wcolumn(k, s):
        return to_src(s, wcol.at[me_s], wcol.at[me_s], css.at[k], crs.at[k])

    def wall(k, d):
        return to_dst(d, wfin.at[me_d], wfin.at[me_d], ass.at[k], ars.at[k])

    loads = [
        pltpu.make_async_copy(a, b, ins.at[i])
        for i, (a, b) in enumerate((
            (x_hbm, xs.at[me_d]), (pos_hbm, pos_ref), (ew_hbm, ew_ref),
            (w_hbm, w_ref), (b_hbm, b_ref), (go_hbm, go_ref),
        ))
    ]
    for c in loads:
        c.start()

    barrier = pltpu.get_barrier_semaphore()

    def greet_src(k, s):
        pl.semaphore_signal(barrier, inc=1, device_id=(s, me_d), device_id_type=pl.DeviceIdType.MESH)

    def greet_dst(k, d):
        pl.semaphore_signal(barrier, inc=1, device_id=(me_s, d), device_id_type=pl.DeviceIdType.MESH)

    src_peers(greet_src)
    dst_peers(greet_dst)
    pl.semaphore_wait(barrier, n_src + n_dst - 2)

    dst_peers(lambda k, d: feat(k, d).start())

    loads[1].wait()
    loads[2].wait()

    group = math.gcd(slots, 16)
    turns = slots // group
    eb = group * edges
    lane = lax.broadcasted_iota(jnp.int32, (1, edges), 1)

    def group_slots(turn):
        if turns == 1:
            return slice(None)
        return pl.ds(pl.multiple_of(turn * group, group), group)

    def build(turn):
        at = group_slots(turn)
        pos = pos_ref[0, 0, at, :]
        weights = ew_ref[0, 0, at, :].astype(F32)
        across = lax.broadcasted_iota(jnp.int32, (edges, TILE), 1)
        turned = pos.T
        tgt, src, wgt = [], [], []
        for j in range(group):
            t = turn * group + j
            tid = tid_ref[0, 0, t]
            p = pos[j : j + 1, :]
            tgt.append(lax.shift_right_logical(p, 7) + lax.div(tid, n_dst) * TILE)
            src.append((p & 127) + lax.rem(tid, n_dst) * TILE)
            wgt.append(jnp.where(lane < cnt_ref[0, 0, t], weights[j : j + 1, :], 0.0))
            c = turned[:, j : j + 1]
            hot_s[j] = jnp.where((c & 127) == across, 1.0, 0.0).astype(BF16)
            hot_t[j] = jnp.where(lax.shift_right_logical(c, 7) == across, 1.0, 0.0).astype(BF16)
        tgt = jnp.concatenate(tgt, axis=1)
        src = jnp.concatenate(src, axis=1)
        wgt = jnp.concatenate(wgt, axis=1)
        spot = lax.broadcasted_iota(jnp.int32, (TILE, eb), 0)

        def col_hot(c):
            ct[rows(c), :] = jnp.where(spot == src - c * TILE, wgt, 0.0).astype(BF16)

        def row_hot(r):
            rt[rows(r), :] = jnp.where(spot == tgt - r * TILE, wgt, 0.0).astype(BF16)

        for n, f in ((n_src, row_hot), (n_dst, col_hot)):
            if n <= 8:
                for i in range(n):
                    f(i)
            else:
                pl.loop(0, n)(f)

    def gather(turn, hot, table, tile_of):
        for j in range(group):
            i = tile_of(tid_ref[0, 0, turn * group + j])
            block = table[i]
            picked[j * edges : (j + 1) * edges, :] = jnp.dot(
                hot[j], block, preferred_element_type=F32
            ).astype(BF16)

    def spread(hot, i):
        return jnp.dot(hot[rows(i), :], picked[...], preferred_element_type=F32)

    def all_turns(hot, table, tile_of, scatter, acc, n):
        acc[...] = jnp.zeros_like(acc)

        @pl.loop(0, turns)
        def _(turn):
            build(turn)
            gather(turn, hot, table, tile_of)

            @pl.loop(0, n)
            def _(i):
                acc[i] += spread(scatter, i)

    if turns == 1:
        build(0)
    for c in loads[3:]:
        c.wait()
    wt[...] = w_ref[...].astype(F32).T.astype(BF16)
    loads[0].wait()
    dst_peers(lambda k, d: feat(k, d).wait_recv())
    if turns == 1:
        gather(0, hot_s, xs, lambda tid: lax.rem(tid, n_dst))
    else:
        all_turns(hot_s, xs, lambda tid: lax.rem(tid, n_dst), rt, facc, n_src)

    def partial_rows(s):
        return spread(rt, s) if turns == 1 else facc[s]

    def send_part(k, s):
        bsend[k] = partial_rows(s).astype(BF16)
        part(k, s).start()

    if relay:
        for k in (5, 7, 6, 3, 2, 1):
            send_part(k, flip(me_s, k))
        far = partial_rows(flip(me_s, 4))
        part(5, me_s).wait_recv()
        bsend[4] = (far + brecv[5].astype(F32)).astype(BF16)
        part(4, flip(me_s, 4)).start()
    else:
        src_peers(send_part)
    agg = partial_rows(me_s)
    if relay:
        for k in (1, 2, 3, 6, 7, 4):
            part(k, flip(me_s, k)).wait_recv()
            agg = agg + brecv[k].astype(F32)
    else:

        def take(k, a):
            part(k, lax.rem(me_s + k, n_src)).wait_recv()
            return a + brecv[k].astype(F32)

        agg = lax.fori_loop(1, n_src, take, agg)
    agg = agg.astype(BF16)

    preact = jnp.dot(agg, w_ref[...], preferred_element_type=F32) + b_ref[...]
    sig = jax.nn.sigmoid(preact)
    gp = (go_ref[...].astype(F32) * sig * (1.0 + preact * (1.0 - sig))).astype(BF16)
    gall[me_s] = jnp.dot(gp, wt[...], preferred_element_type=F32).astype(BF16)
    if relay:
        for k in (4, 7, 6, 3, 2, 1):
            back(k, flip(me_s, k)).start()
    else:
        src_peers(lambda k, s: back(k, s).start())
    hid_ref[...] = (preact * sig).astype(BF16)

    dw = jnp.dot(agg.astype(F32).T.astype(BF16), gp, preferred_element_type=F32)
    bs = jnp.sum(gp.astype(F32), axis=0, keepdims=True)
    sub = lax.broadcasted_iota(jnp.int32, (8, 128), 0)
    bv = jnp.where(sub == 0, bs[:, :128], jnp.where(sub == 1, bs[:, 128:], 0.0))
    units = []
    for q in range(UNITS):
        i, h = q // 2, q % 2
        units.append(dw[8 * i : 8 * i + 8, 128 * h : 128 * h + 128])
    for d in range(n_dst):
        chunk = jnp.concatenate(units[d * ud : d * ud + ud] + [bv, jnp.zeros_like(bv)], axis=0)
        wsend[d] = chunk.astype(BF16)
    drecv[me_d] = wsend[me_d]
    dst_peers(lambda k, d: wdst(k, d).start())

    if relay:
        back(4, flip(me_s, 4)).wait_recv()
        back(5, me_s).start()

    def ordered(ref, n):
        total = ref[0].astype(F32)
        for i in range(1, n):
            total = total + ref[i].astype(F32)
        return total

    scale = 1.0 / math.sqrt(TILE * n_src * n_dst)
    dst_peers(lambda k, d: wdst(k, d).wait_recv())
    chunk = ordered(drecv, n_dst).reshape(ud + 2, 8, 128)[: ud + 1]
    if pu:
        for s in range(n_src):
            ssend[s, :pu] = chunk[s * pu : s * pu + pu]
            ssend[s, pu] = chunk[ud]
        srecv[me_s] = ssend[me_s]
    else:
        ssend[0] = chunk
        srecv[me_s] = chunk
    src_peers(lambda k, s: wsrc(k, s).start())
    if relay:
        for k in (1, 2, 3, 6, 7, 5):
            back(k, flip(me_s, k)).wait_recv()
    else:
        src_peers(lambda k, s: back(k, s).wait_recv())

    if turns == 1:
        gather(0, hot_t, gall, lambda tid: lax.div(tid, n_dst))
    else:
        all_turns(hot_t, gall, lambda tid: lax.div(tid, n_dst), ct, bacc, n_dst)

    def back_rows(d):
        return spread(ct, d) if turns == 1 else bacc[d]

    def send_fin(k, d):
        fsend[k] = back_rows(d).astype(BF16)
        fin(k, d).start()

    dst_peers(send_fin)

    src_peers(lambda k, s: wsrc(k, s).wait_recv())
    total = ordered(srecv, n_src) * scale
    if pu:
        wcol[me_s] = total[:pu]
        src_peers(lambda k, s: wcolumn(k, s).start())
    own = back_rows(me_d)

    if pu:
        src_peers(lambda k, s: wcolumn(k, s).wait_recv())
        wfin[me_d] = wcol[...].reshape(ud * 8, 128).astype(BF16)
    else:
        wfin[me_d] = total[:ud].reshape(ud * 8, 128).astype(BF16)
    dst_peers(lambda k, d: wall(k, d).start())
    last = -1
    bg_ref[:, :128] = total[last, 0:1, :]
    bg_ref[:, 128:] = total[last, 1:2, :]

    for k in range(n_dst - 1, 0, -1):
        fin(k, me_d).wait_recv()
        own = own + frecv[k].astype(F32)
    ig_ref[...] = own.astype(BF16)

    dst_peers(lambda k, d: wall(k, d).wait_recv())
    for q in range(UNITS):
        i, h = q // 2, q % 2
        at = 8 * (q % ud)
        wg_ref[8 * i : 8 * i + 8, 128 * h : 128 * h + 128] = wfin[q // ud, at : at + 8, :].astype(F32)

    src_copies = (part, back, wsrc, wcolumn) if pu else (part, back, wsrc)
    for c in (feat, fin, wdst, wall):
        dst_peers(lambda k, p, c=c: c(k, p).wait_send())
    for c in src_copies:
        src_peers(lambda k, p, c=c: c(k, p).wait_send())


def store(h_in, i_in, w_in, b_in, h_out, i_out, w_out, b_out, sems):
    pairs = ((h_in, h_out), (i_in, i_out), (w_in, w_out), (b_in, b_out))
    copies = [pltpu.make_async_copy(a, b, sems.at[i]) for i, (a, b) in enumerate(pairs)]
    for c in copies:
        c.start()
    for c in copies:
        c.wait()


def body(n_src, n_dst, features, weight, bias, tile_index, edge_count, edge_pos, edge_weight, grad_out):
    slots, edges = edge_pos.shape[2], edge_pos.shape[3]
    own = features.shape[0]
    group = math.gcd(slots, 16)
    eb = group * edges
    many = slots > group
    ud = UNITS // n_dst
    pu = ud // n_src
    vm = pl.BlockSpec(memory_space=pltpu.VMEM)
    sm = pl.BlockSpec(memory_space=pltpu.SMEM)
    hbm = pl.BlockSpec(memory_space=pltpu.HBM)
    anyw = pl.BlockSpec(memory_space=pl.ANY)
    dma = pltpu.SemaphoreType.DMA
    s_sems = [dma((n_src,)), dma((n_src,))]
    d_sems = [dma((n_dst,)), dma((n_dst,))]
    outs = (
        jax.ShapeDtypeStruct((own, F_HID), BF16),
        jax.ShapeDtypeStruct((own, F_IN), BF16),
        jax.ShapeDtypeStruct((F_IN, F_HID), F32),
        jax.ShapeDtypeStruct((1, F_HID), F32),
    )
    arrays = (features, weight, bias.reshape(1, -1), edge_pos, edge_weight, grad_out)
    piece = (pu or ud) + 1
    results = pl.pallas_call(
        functools.partial(kernel, n_src, n_dst, slots, edges),
        out_shape=tuple(pltpu.VMEM(o.shape, o.dtype) for o in outs),
        in_specs=[sm, sm, *[hbm] * 6],
        out_specs=(vm,) * 4,
        scratch_shapes=[
            *[pltpu.VMEM(a.shape, a.dtype) for a in arrays[1:]],
            pltpu.VMEM((n_dst, TILE, F_IN), BF16),
            pltpu.VMEM((n_src * TILE, eb), BF16),
            pltpu.VMEM((n_dst * TILE, eb), BF16),
            pltpu.VMEM((group, edges, TILE), BF16),
            pltpu.VMEM((group, edges, TILE), BF16),
            pltpu.VMEM((eb, F_IN), BF16),
            pltpu.VMEM((n_src if many else 1, TILE, F_IN), F32),
            pltpu.VMEM((n_dst if many else 1, TILE, F_IN), F32),
            pltpu.VMEM((F_HID, F_IN), BF16),
            pltpu.VMEM((n_src, TILE, F_IN), BF16),
            pltpu.VMEM((n_src, TILE, F_IN), BF16),
            pltpu.VMEM((n_src, TILE, F_IN), BF16),
            pltpu.VMEM((n_dst, TILE, F_IN), BF16),
            pltpu.VMEM((n_dst, TILE, F_IN), BF16),
            pltpu.VMEM((n_dst, (ud + 2) * 8, 128), BF16),
            pltpu.VMEM((n_dst, (ud + 2) * 8, 128), BF16),
            pltpu.VMEM((n_src if pu else 1, piece, 8, 128), F32),
            pltpu.VMEM((n_src, piece, 8, 128), F32),
            pltpu.VMEM((n_src, max(pu, 1), 8, 128), F32),
            pltpu.VMEM((n_dst, ud * 8, 128), BF16),
            dma((len(arrays),)),
            *d_sems, *s_sems, *s_sems, *d_sems, *d_sems, *s_sems, *s_sems, *d_sems,
        ],
        compiler_params=pltpu.CompilerParams(
            collective_id=0, has_side_effects=True,
            vmem_limit_bytes=(64 << 20) - (1024 << 10),
        ),
    )(tile_index, edge_count, *arrays)
    hidden, input_grad, weight_grad, bias_grad = pl.pallas_call(
        store,
        out_shape=outs,
        in_specs=[vm] * 4,
        out_specs=(anyw,) * 4,
        scratch_shapes=[dma((4,))],
        compiler_params=pltpu.CompilerParams(vmem_limit_bytes=4 << 20),
    )(*results)
    return hidden, input_grad, weight_grad, bias_grad.reshape(-1)


def solution(mesh):
    placed = (
        P(("src", "dst"), None),
        P(),
        P(),
        P("src", "dst", None),
        P("src", "dst", None),
        P("src", "dst", None, None),
        P("src", "dst", None, None),
        P(("src", "dst"), None),
    )
    return jax.shard_map(
        functools.partial(body, mesh.shape["src"], mesh.shape["dst"]),
        mesh=mesh,
        in_specs=placed,
        out_specs=(P(("src", "dst"), None), P(("src", "dst"), None), P(), P()),
        check_vma=False,
    )
```

```python
import functools
import math

import jax
import jax.numpy as jnp
from jax import lax
from jax.experimental import pallas as pl
from jax.experimental.pallas import tpu as pltpu
from jax.sharding import PartitionSpec as P

TILE = 128
F_IN = 128
F_HID = 256
UNITS = 32
F32 = jnp.float32
BF16 = jnp.bfloat16


def flip(me, k):
    out = me
    bit = 1
    while bit <= k:
        if k & bit:
            out = out + bit * (1 - 2 * (lax.div(me, bit) % 2))
        bit *= 2
    return out


def each_peer(n, me, body):
    if n <= 8:
        for k in range(n - 1, 0, -1):
            body(k, flip(me, k))
    else:

        def step(k, carry):
            body(k, lax.rem(me + k, n))
            return carry

        lax.fori_loop(1, n, step, 0)


def rows(i, n=TILE):
    return pl.ds(pl.multiple_of(i * n, n), n)


def kernel(
    n_src, n_dst, slots, edges,
    tid_ref, cnt_ref, x_hbm, w_hbm, b_hbm, pos_hbm, ew_hbm, go_hbm,
    hid_ref, ig_ref, wg_ref, bg_ref,
    w_ref, b_ref, pos_ref, ew_ref, go_ref,
    xs, rt, ct, hot_s, hot_t, picked, facc, bacc, wt, bsend, brecv, gall, fsend, frecv,
    wsend, wrecv, drecv, wfin,
    ins, xss, xrs, bss, brs, gss, grs, fss, frs, wss, wrs, dss, drs, ass, ars,
):
    me_s = lax.axis_index("src")
    me_d = lax.axis_index("dst")
    per = UNITS // n_src
    piece = wsend.shape[1]
    src_peers = functools.partial(each_peer, n_src, me_s)
    dst_peers = functools.partial(each_peer, n_dst, me_d)

    def to_src(s, src, dst, ss, rs):
        return pltpu.make_async_remote_copy(
            src_ref=src, dst_ref=dst, send_sem=ss, recv_sem=rs,
            device_id=(s, me_d), device_id_type=pl.DeviceIdType.MESH,
        )

    def to_dst(d, src, dst, ss, rs):
        return pltpu.make_async_remote_copy(
            src_ref=src, dst_ref=dst, send_sem=ss, recv_sem=rs,
            device_id=(me_s, d), device_id_type=pl.DeviceIdType.MESH,
        )

    def feat(k, d):
        return to_dst(d, x_hbm, xs.at[me_d], xss.at[k], xrs.at[k])

    def part(k, s):
        return to_src(s, bsend.at[k], brecv.at[k], bss.at[k], brs.at[k])

    def back(k, s):
        return to_src(s, gall.at[me_s], gall.at[me_s], gss.at[k], grs.at[k])

    def fin(k, d):
        return to_dst(d, fsend.at[k], frecv.at[k], fss.at[k], frs.at[k])

    def wsrc(k, s):
        return to_src(s, wsend.at[s], wrecv.at[me_s], wss.at[k], wrs.at[k])

    def wdst(k, d):
        return to_dst(d, drecv.at[me_d], drecv.at[me_d], dss.at[k], drs.at[k])

    def wall(k, s):
        return to_src(s, wfin.at[me_s], wfin.at[me_s], ass.at[k], ars.at[k])

    loads = [
        pltpu.make_async_copy(a, b, ins.at[i])
        for i, (a, b) in enumerate((
            (x_hbm, xs.at[me_d]), (pos_hbm, pos_ref), (ew_hbm, ew_ref),
            (w_hbm, w_ref), (b_hbm, b_ref), (go_hbm, go_ref),
        ))
    ]
    for c in loads:
        c.start()

    barrier = pltpu.get_barrier_semaphore()

    def greet_src(k, s):
        pl.semaphore_signal(barrier, inc=1, device_id=(s, me_d), device_id_type=pl.DeviceIdType.MESH)

    def greet_dst(k, d):
        pl.semaphore_signal(barrier, inc=1, device_id=(me_s, d), device_id_type=pl.DeviceIdType.MESH)

    src_peers(greet_src)
    dst_peers(greet_dst)
    pl.semaphore_wait(barrier, n_src + n_dst - 2)

    dst_peers(lambda k, d: feat(k, d).start())

    loads[1].wait()
    loads[2].wait()

    group = math.gcd(slots, 16)
    turns = slots // group
    eb = group * edges
    lane = lax.broadcasted_iota(jnp.int32, (1, edges), 1)

    def group_slots(turn):
        if turns == 1:
            return slice(None)
        return pl.ds(pl.multiple_of(turn * group, group), group)

    def build(turn):
        at = group_slots(turn)
        pos = pos_ref[0, 0, at, :]
        weights = ew_ref[0, 0, at, :].astype(F32)
        across = lax.broadcasted_iota(jnp.int32, (edges, TILE), 1)
        turned = pos.T
        tgt, src, wgt = [], [], []
        for j in range(group):
            t = turn * group + j
            tid = tid_ref[0, 0, t]
            p = pos[j : j + 1, :]
            tgt.append(lax.shift_right_logical(p, 7) + lax.div(tid, n_dst) * TILE)
            src.append((p & 127) + lax.rem(tid, n_dst) * TILE)
            wgt.append(jnp.where(lane < cnt_ref[0, 0, t], weights[j : j + 1, :], 0.0))
            c = turned[:, j : j + 1]
            hot_s[j] = jnp.where((c & 127) == across, 1.0, 0.0).astype(BF16)
            hot_t[j] = jnp.where(lax.shift_right_logical(c, 7) == across, 1.0, 0.0).astype(BF16)
        tgt = jnp.concatenate(tgt, axis=1)
        src = jnp.concatenate(src, axis=1)
        wgt = jnp.concatenate(wgt, axis=1)
        spot = lax.broadcasted_iota(jnp.int32, (TILE, eb), 0)

        def col_hot(c):
            ct[rows(c), :] = jnp.where(spot == src - c * TILE, wgt, 0.0).astype(BF16)

        def row_hot(r):
            rt[rows(r), :] = jnp.where(spot == tgt - r * TILE, wgt, 0.0).astype(BF16)

        for n, f in ((n_src, row_hot), (n_dst, col_hot)):
            if n <= 8:
                for i in range(n):
                    f(i)
            else:
                pl.loop(0, n)(f)

    def gather(turn, hot, table, tile_of):
        for j in range(group):
            i = tile_of(tid_ref[0, 0, turn * group + j])
            block = table[i]
            picked[j * edges : (j + 1) * edges, :] = jnp.dot(
                hot[j], block, preferred_element_type=F32
            ).astype(BF16)

    def spread(hot, i):
        return jnp.dot(hot[rows(i), :], picked[...], preferred_element_type=F32)

    def all_turns(hot, table, tile_of, scatter, acc, n):
        acc[...] = jnp.zeros_like(acc)

        @pl.loop(0, turns)
        def _(turn):
            build(turn)
            gather(turn, hot, table, tile_of)

            @pl.loop(0, n)
            def _(i):
                acc[i] += spread(scatter, i)

    if turns == 1:
        build(0)
    for c in loads[3:]:
        c.wait()
    wt[...] = w_ref[...].astype(F32).T.astype(BF16)
    loads[0].wait()
    dst_peers(lambda k, d: feat(k, d).wait_recv())
    if turns == 1:
        gather(0, hot_s, xs, lambda tid: lax.rem(tid, n_dst))
    else:
        all_turns(hot_s, xs, lambda tid: lax.rem(tid, n_dst), rt, facc, n_src)

    def partial_rows(s):
        return spread(rt, s) if turns == 1 else facc[s]

    def send_part(k, s):
        bsend[k] = partial_rows(s).astype(BF16)
        part(k, s).start()

    src_peers(send_part)
    agg = partial_rows(me_s)
    if n_src <= 8:
        for k in range(1, n_src):
            part(k, flip(me_s, k)).wait_recv()
            agg = agg + brecv[k].astype(F32)
    else:

        def take(k, a):
            part(k, lax.rem(me_s + k, n_src)).wait_recv()
            return a + brecv[k].astype(F32)

        agg = lax.fori_loop(1, n_src, take, agg)
    agg = agg.astype(BF16)

    preact = jnp.dot(agg, w_ref[...], preferred_element_type=F32) + b_ref[...]
    sig = jax.nn.sigmoid(preact)
    gp = (go_ref[...].astype(F32) * sig * (1.0 + preact * (1.0 - sig))).astype(BF16)
    gall[me_s] = jnp.dot(gp, wt[...], preferred_element_type=F32).astype(BF16)
    src_peers(lambda k, s: back(k, s).start())
    hid_ref[...] = (preact * sig).astype(BF16)

    dw = jnp.dot(agg.astype(F32).T.astype(BF16), gp, preferred_element_type=F32)
    bs = jnp.sum(gp.astype(F32), axis=0, keepdims=True)
    sub = lax.broadcasted_iota(jnp.int32, (8, 128), 0)
    bv = jnp.where(sub == 0, bs[:, :128], jnp.where(sub == 1, bs[:, 128:], 0.0))
    units = []
    for q in range(UNITS):
        i, h = q // 2, q % 2
        units.append(dw[8 * i : 8 * i + 8, 128 * h : 128 * h + 128])
    fill = [jnp.zeros_like(bv)] * (piece // 8 - per - 1)
    for s in range(n_src):
        wsend[s] = jnp.concatenate(units[s * per : s * per + per] + [bv] + fill, axis=0).astype(BF16)
    wrecv[me_s] = wsend[me_s]
    src_peers(lambda k, s: wsrc(k, s).start())

    def ordered(ref, n):
        total = ref[0].astype(F32)
        for i in range(1, n):
            total = total + ref[i].astype(F32)
        return total

    scale = 1.0 / math.sqrt(TILE * n_src * n_dst)
    src_peers(lambda k, s: back(k, s).wait_recv())

    if turns == 1:
        gather(0, hot_t, gall, lambda tid: lax.div(tid, n_dst))
    else:
        all_turns(hot_t, gall, lambda tid: lax.div(tid, n_dst), ct, bacc, n_dst)

    def back_rows(d):
        return spread(ct, d) if turns == 1 else bacc[d]

    def send_fin(k, d):
        fsend[k] = back_rows(d).astype(BF16)
        fin(k, d).start()

    dst_peers(send_fin)

    src_peers(lambda k, s: wsrc(k, s).wait_recv())
    drecv[me_d] = ordered(wrecv, n_src).astype(BF16)
    dst_peers(lambda k, d: wdst(k, d).start())
    own = back_rows(me_d)
    dst_peers(lambda k, d: wdst(k, d).wait_recv())
    total = ordered(drecv, n_dst) * scale
    wfin[me_s] = total.astype(BF16)
    src_peers(lambda k, s: wall(k, s).start())
    bg_ref[:, :128] = total[per * 8 : per * 8 + 1, :]
    bg_ref[:, 128:] = total[per * 8 + 1 : per * 8 + 2, :]

    for k in range(n_dst - 1, 0, -1):
        fin(k, me_d).wait_recv()
        own = own + frecv[k].astype(F32)
    ig_ref[...] = own.astype(BF16)

    src_peers(lambda k, s: wall(k, s).wait_recv())
    for q in range(UNITS):
        i, h = q // 2, q % 2
        at = 8 * (q % per)
        wg_ref[8 * i : 8 * i + 8, 128 * h : 128 * h + 128] = wfin[q // per, at : at + 8, :].astype(F32)

    for c in (feat, fin, wdst):
        dst_peers(lambda k, p, c=c: c(k, p).wait_send())
    for c in (part, back, wsrc, wall):
        src_peers(lambda k, p, c=c: c(k, p).wait_send())


def store(h_in, i_in, w_in, b_in, h_out, i_out, w_out, b_out, sems):
    pairs = ((h_in, h_out), (i_in, i_out), (w_in, w_out), (b_in, b_out))
    copies = [pltpu.make_async_copy(a, b, sems.at[i]) for i, (a, b) in enumerate(pairs)]
    for c in copies:
        c.start()
    for c in copies:
        c.wait()


def body(n_src, n_dst, features, weight, bias, tile_index, edge_count, edge_pos, edge_weight, grad_out):
    slots, edges = edge_pos.shape[2], edge_pos.shape[3]
    own = features.shape[0]
    group = math.gcd(slots, 16)
    eb = group * edges
    many = slots > group
    per = UNITS // n_src
    piece = (per // 2 + 1) * 16
    vm = pl.BlockSpec(memory_space=pltpu.VMEM)
    sm = pl.BlockSpec(memory_space=pltpu.SMEM)
    hbm = pl.BlockSpec(memory_space=pltpu.HBM)
    anyw = pl.BlockSpec(memory_space=pl.ANY)
    dma = pltpu.SemaphoreType.DMA
    s_sems = [dma((n_src,)), dma((n_src,))]
    d_sems = [dma((n_dst,)), dma((n_dst,))]
    outs = (
        jax.ShapeDtypeStruct((own, F_HID), BF16),
        jax.ShapeDtypeStruct((own, F_IN), BF16),
        jax.ShapeDtypeStruct((F_IN, F_HID), F32),
        jax.ShapeDtypeStruct((1, F_HID), F32),
    )
    arrays = (features, weight, bias.reshape(1, -1), edge_pos, edge_weight, grad_out)
    results = pl.pallas_call(
        functools.partial(kernel, n_src, n_dst, slots, edges),
        out_shape=tuple(pltpu.VMEM(o.shape, o.dtype) for o in outs),
        in_specs=[sm, sm, *[hbm] * 6],
        out_specs=(vm,) * 4,
        scratch_shapes=[
            *[pltpu.VMEM(a.shape, a.dtype) for a in arrays[1:]],
            pltpu.VMEM((n_dst, TILE, F_IN), BF16),
            pltpu.VMEM((n_src * TILE, eb), BF16),
            pltpu.VMEM((n_dst * TILE, eb), BF16),
            pltpu.VMEM((group, edges, TILE), BF16),
            pltpu.VMEM((group, edges, TILE), BF16),
            pltpu.VMEM((eb, F_IN), BF16),
            pltpu.VMEM((n_src if many else 1, TILE, F_IN), F32),
            pltpu.VMEM((n_dst if many else 1, TILE, F_IN), F32),
            pltpu.VMEM((F_HID, F_IN), BF16),
            pltpu.VMEM((n_src, TILE, F_IN), BF16),
            pltpu.VMEM((n_src, TILE, F_IN), BF16),
            pltpu.VMEM((n_src, TILE, F_IN), BF16),
            pltpu.VMEM((n_dst, TILE, F_IN), BF16),
            pltpu.VMEM((n_dst, TILE, F_IN), BF16),
            pltpu.VMEM((n_src, piece, 128), BF16),
            pltpu.VMEM((n_src, piece, 128), BF16),
            pltpu.VMEM((n_dst, piece, 128), BF16),
            pltpu.VMEM((n_src, piece, 128), BF16),
            dma((len(arrays),)),
            *d_sems, *s_sems, *s_sems, *d_sems, *s_sems, *d_sems, *s_sems,
        ],
        compiler_params=pltpu.CompilerParams(
            collective_id=0, has_side_effects=True,
            vmem_limit_bytes=(64 << 20) - (1024 << 10),
        ),
    )(tile_index, edge_count, *arrays)
    hidden, input_grad, weight_grad, bias_grad = pl.pallas_call(
        store,
        out_shape=outs,
        in_specs=[vm] * 4,
        out_specs=(anyw,) * 4,
        scratch_shapes=[dma((4,))],
        compiler_params=pltpu.CompilerParams(vmem_limit_bytes=4 << 20),
    )(*results)
    return hidden, input_grad, weight_grad, bias_grad.reshape(-1)


def solution(mesh):
    placed = (
        P(("src", "dst"), None),
        P(),
        P(),
        P("src", "dst", None),
        P("src", "dst", None),
        P("src", "dst", None, None),
        P("src", "dst", None, None),
        P(("src", "dst"), None),
    )
    return jax.shard_map(
        functools.partial(body, mesh.shape["src"], mesh.shape["dst"]),
        mesh=mesh,
        in_specs=placed,
        out_specs=(P(("src", "dst"), None), P(("src", "dst"), None), P(), P()),
        check_vma=False,
    )
```

```python
import functools
import math

import jax
import jax.numpy as jnp
from jax import lax
from jax.experimental import pallas as pl
from jax.experimental.pallas import tpu as pltpu
from jax.sharding import PartitionSpec as P

TILE = 128
F_IN = 128
F_HID = 256
UNITS = 32
F32 = jnp.float32
BF16 = jnp.bfloat16


def flip(me, k):
    out = me
    bit = 1
    while bit <= k:
        if k & bit:
            out = out + bit * (1 - 2 * (lax.div(me, bit) % 2))
        bit *= 2
    return out


def each_peer(n, me, body):
    if n <= 8:
        for k in range(n - 1, 0, -1):
            body(k, flip(me, k))
    else:

        def step(k, carry):
            body(k, lax.rem(me + k, n))
            return carry

        lax.fori_loop(1, n, step, 0)


def rows(i, n=TILE):
    return pl.ds(pl.multiple_of(i * n, n), n)


def kernel(
    n_src, n_dst, slots, edges,
    tid_ref, cnt_ref, x_hbm, w_hbm, b_hbm, pos_hbm, ew_hbm, go_hbm,
    hid_ref, ig_ref, wg_ref, bg_ref,
    w_ref, b_ref, pos_ref, ew_ref, go_ref,
    xs, rt, ct, hot_s, hot_t, picked, facc, bacc, wt, bsend, brecv, gall, fsend, frecv,
    wsend, drecv, ssend, srecv, wcol, wfin,
    ins, xss, xrs, bss, brs, gss, grs, fss, frs, dss, drs, wss, wrs, css, crs, ass, ars,
):
    me_s = lax.axis_index("src")
    me_d = lax.axis_index("dst")
    ud = UNITS // n_dst
    pu = ud // n_src
    src_peers = functools.partial(each_peer, n_src, me_s)
    dst_peers = functools.partial(each_peer, n_dst, me_d)

    def to_src(s, src, dst, ss, rs):
        return pltpu.make_async_remote_copy(
            src_ref=src, dst_ref=dst, send_sem=ss, recv_sem=rs,
            device_id=(s, me_d), device_id_type=pl.DeviceIdType.MESH,
        )

    def to_dst(d, src, dst, ss, rs):
        return pltpu.make_async_remote_copy(
            src_ref=src, dst_ref=dst, send_sem=ss, recv_sem=rs,
            device_id=(me_s, d), device_id_type=pl.DeviceIdType.MESH,
        )

    def feat(k, d):
        return to_dst(d, x_hbm, xs.at[me_d], xss.at[k], xrs.at[k])

    def part(k, s):
        return to_src(s, bsend.at[k], brecv.at[k], bss.at[k], brs.at[k])

    def back(k, s):
        return to_src(s, gall.at[me_s], gall.at[me_s], gss.at[k], grs.at[k])

    def fin(k, d):
        return to_dst(d, fsend.at[k], frecv.at[k], fss.at[k], frs.at[k])

    def wdst(k, d):
        return to_dst(d, wsend.at[d], drecv.at[me_d], dss.at[k], drs.at[k])

    def wsrc(k, s):
        return to_src(s, ssend.at[s if pu else 0], srecv.at[me_s], wss.at[k], wrs.at[k])

    def wcolumn(k, s):
        return to_src(s, wcol.at[me_s], wcol.at[me_s], css.at[k], crs.at[k])

    def wall(k, d):
        return to_dst(d, wfin.at[me_d], wfin.at[me_d], ass.at[k], ars.at[k])

    loads = [
        pltpu.make_async_copy(a, b, ins.at[i])
        for i, (a, b) in enumerate((
            (x_hbm, xs.at[me_d]), (pos_hbm, pos_ref), (ew_hbm, ew_ref),
            (w_hbm, w_ref), (b_hbm, b_ref), (go_hbm, go_ref),
        ))
    ]
    for c in loads:
        c.start()

    barrier = pltpu.get_barrier_semaphore()

    def greet_src(k, s):
        pl.semaphore_signal(barrier, inc=1, device_id=(s, me_d), device_id_type=pl.DeviceIdType.MESH)

    def greet_dst(k, d):
        pl.semaphore_signal(barrier, inc=1, device_id=(me_s, d), device_id_type=pl.DeviceIdType.MESH)

    src_peers(greet_src)
    dst_peers(greet_dst)
    pl.semaphore_wait(barrier, n_src + n_dst - 2)

    dst_peers(lambda k, d: feat(k, d).start())

    loads[1].wait()
    loads[2].wait()

    group = math.gcd(slots, 16)
    turns = slots // group
    eb = group * edges
    lane = lax.broadcasted_iota(jnp.int32, (1, edges), 1)

    def group_slots(turn):
        if turns == 1:
            return slice(None)
        return pl.ds(pl.multiple_of(turn * group, group), group)

    def build(turn):
        at = group_slots(turn)
        pos = pos_ref[0, 0, at, :]
        weights = ew_ref[0, 0, at, :].astype(F32)
        across = lax.broadcasted_iota(jnp.int32, (edges, TILE), 1)
        turned = pos.T
        tgt, src, wgt = [], [], []
        for j in range(group):
            t = turn * group + j
            tid = tid_ref[0, 0, t]
            p = pos[j : j + 1, :]
            tgt.append(lax.shift_right_logical(p, 7) + lax.div(tid, n_dst) * TILE)
            src.append((p & 127) + lax.rem(tid, n_dst) * TILE)
            wgt.append(jnp.where(lane < cnt_ref[0, 0, t], weights[j : j + 1, :], 0.0))
            c = turned[:, j : j + 1]
            hot_s[j] = jnp.where((c & 127) == across, 1.0, 0.0).astype(BF16)
            hot_t[j] = jnp.where(lax.shift_right_logical(c, 7) == across, 1.0, 0.0).astype(BF16)
        tgt = jnp.concatenate(tgt, axis=1)
        src = jnp.concatenate(src, axis=1)
        wgt = jnp.concatenate(wgt, axis=1)
        spot = lax.broadcasted_iota(jnp.int32, (TILE, eb), 0)

        def col_hot(c):
            ct[rows(c), :] = jnp.where(spot == src - c * TILE, wgt, 0.0).astype(BF16)

        def row_hot(r):
            rt[rows(r), :] = jnp.where(spot == tgt - r * TILE, wgt, 0.0).astype(BF16)

        for n, f in ((n_src, row_hot), (n_dst, col_hot)):
            if n <= 8:
                for i in range(n):
                    f(i)
            else:
                pl.loop(0, n)(f)

    def gather(turn, hot, table, tile_of):
        for j in range(group):
            i = tile_of(tid_ref[0, 0, turn * group + j])
            block = table[i]
            picked[j * edges : (j + 1) * edges, :] = jnp.dot(
                hot[j], block, preferred_element_type=F32
            ).astype(BF16)

    def spread(hot, i):
        return jnp.dot(hot[rows(i), :], picked[...], preferred_element_type=F32)

    def all_turns(hot, table, tile_of, scatter, acc, n):
        acc[...] = jnp.zeros_like(acc)

        @pl.loop(0, turns)
        def _(turn):
            build(turn)
            gather(turn, hot, table, tile_of)

            @pl.loop(0, n)
            def _(i):
                acc[i] += spread(scatter, i)

    if turns == 1:
        build(0)
    for c in loads[3:]:
        c.wait()
    wt[...] = w_ref[...].astype(F32).T.astype(BF16)
    loads[0].wait()
    dst_peers(lambda k, d: feat(k, d).wait_recv())
    if turns == 1:
        gather(0, hot_s, xs, lambda tid: lax.rem(tid, n_dst))
    else:
        all_turns(hot_s, xs, lambda tid: lax.rem(tid, n_dst), rt, facc, n_src)

    def partial_rows(s):
        return spread(rt, s) if turns == 1 else facc[s]

    def send_part(k, s):
        bsend[k] = partial_rows(s).astype(BF16)
        part(k, s).start()

    src_peers(send_part)
    agg = partial_rows(me_s)
    if n_src <= 8:
        for k in range(1, n_src):
            part(k, flip(me_s, k)).wait_recv()
            agg = agg + brecv[k].astype(F32)
    else:

        def take(k, a):
            part(k, lax.rem(me_s + k, n_src)).wait_recv()
            return a + brecv[k].astype(F32)

        agg = lax.fori_loop(1, n_src, take, agg)
    agg = agg.astype(BF16)

    preact = jnp.dot(agg, w_ref[...], preferred_element_type=F32) + b_ref[...]
    sig = jax.nn.sigmoid(preact)
    gp = (go_ref[...].astype(F32) * sig * (1.0 + preact * (1.0 - sig))).astype(BF16)
    gall[me_s] = jnp.dot(gp, wt[...], preferred_element_type=F32).astype(BF16)
    src_peers(lambda k, s: back(k, s).start())
    hid_ref[...] = (preact * sig).astype(BF16)

    dw = jnp.dot(agg.astype(F32).T.astype(BF16), gp, preferred_element_type=F32)
    bs = jnp.sum(gp.astype(F32), axis=0, keepdims=True)
    sub = lax.broadcasted_iota(jnp.int32, (8, 128), 0)
    bv = jnp.where(sub == 0, bs[:, :128], jnp.where(sub == 1, bs[:, 128:], 0.0))
    units = []
    for q in range(UNITS):
        i, h = q // 2, q % 2
        units.append(dw[8 * i : 8 * i + 8, 128 * h : 128 * h + 128])
    for d in range(n_dst):
        chunk = jnp.concatenate(units[d * ud : d * ud + ud] + [bv, jnp.zeros_like(bv)], axis=0)
        wsend[d] = chunk.astype(BF16)
    drecv[me_d] = wsend[me_d]
    dst_peers(lambda k, d: wdst(k, d).start())

    def ordered(ref, n):
        total = ref[0].astype(F32)
        for i in range(1, n):
            total = total + ref[i].astype(F32)
        return total

    scale = 1.0 / math.sqrt(TILE * n_src * n_dst)
    dst_peers(lambda k, d: wdst(k, d).wait_recv())
    chunk = ordered(drecv, n_dst).reshape(ud + 2, 8, 128)[: ud + 1]
    if pu:
        for s in range(n_src):
            ssend[s, :pu] = chunk[s * pu : s * pu + pu]
            ssend[s, pu] = chunk[ud]
        srecv[me_s] = ssend[me_s]
    else:
        ssend[0] = chunk
        srecv[me_s] = chunk
    src_peers(lambda k, s: wsrc(k, s).start())
    src_peers(lambda k, s: back(k, s).wait_recv())

    if turns == 1:
        gather(0, hot_t, gall, lambda tid: lax.div(tid, n_dst))
    else:
        all_turns(hot_t, gall, lambda tid: lax.div(tid, n_dst), ct, bacc, n_dst)

    def back_rows(d):
        return spread(ct, d) if turns == 1 else bacc[d]

    def send_fin(k, d):
        fsend[k] = back_rows(d).astype(BF16)
        fin(k, d).start()

    dst_peers(send_fin)

    src_peers(lambda k, s: wsrc(k, s).wait_recv())
    total = ordered(srecv, n_src) * scale
    if pu:
        wcol[me_s] = total[:pu]
        src_peers(lambda k, s: wcolumn(k, s).start())
    own = back_rows(me_d)

    if pu:
        src_peers(lambda k, s: wcolumn(k, s).wait_recv())
        wfin[me_d] = wcol[...].reshape(ud * 8, 128).astype(BF16)
    else:
        wfin[me_d] = total[:ud].reshape(ud * 8, 128).astype(BF16)
    dst_peers(lambda k, d: wall(k, d).start())
    last = -1
    bg_ref[:, :128] = total[last, 0:1, :]
    bg_ref[:, 128:] = total[last, 1:2, :]

    for k in range(n_dst - 1, 0, -1):
        fin(k, me_d).wait_recv()
        own = own + frecv[k].astype(F32)
    ig_ref[...] = own.astype(BF16)

    dst_peers(lambda k, d: wall(k, d).wait_recv())
    for q in range(UNITS):
        i, h = q // 2, q % 2
        at = 8 * (q % ud)
        wg_ref[8 * i : 8 * i + 8, 128 * h : 128 * h + 128] = wfin[q // ud, at : at + 8, :].astype(F32)

    src_copies = (part, back, wsrc, wcolumn) if pu else (part, back, wsrc)
    for c in (feat, fin, wdst, wall):
        dst_peers(lambda k, p, c=c: c(k, p).wait_send())
    for c in src_copies:
        src_peers(lambda k, p, c=c: c(k, p).wait_send())


def store(h_in, i_in, w_in, b_in, h_out, i_out, w_out, b_out, sems):
    pairs = ((h_in, h_out), (i_in, i_out), (w_in, w_out), (b_in, b_out))
    copies = [pltpu.make_async_copy(a, b, sems.at[i]) for i, (a, b) in enumerate(pairs)]
    for c in copies:
        c.start()
    for c in copies:
        c.wait()


def body(n_src, n_dst, features, weight, bias, tile_index, edge_count, edge_pos, edge_weight, grad_out):
    slots, edges = edge_pos.shape[2], edge_pos.shape[3]
    own = features.shape[0]
    group = math.gcd(slots, 16)
    eb = group * edges
    many = slots > group
    ud = UNITS // n_dst
    pu = ud // n_src
    vm = pl.BlockSpec(memory_space=pltpu.VMEM)
    sm = pl.BlockSpec(memory_space=pltpu.SMEM)
    hbm = pl.BlockSpec(memory_space=pltpu.HBM)
    anyw = pl.BlockSpec(memory_space=pl.ANY)
    dma = pltpu.SemaphoreType.DMA
    s_sems = [dma((n_src,)), dma((n_src,))]
    d_sems = [dma((n_dst,)), dma((n_dst,))]
    outs = (
        jax.ShapeDtypeStruct((own, F_HID), BF16),
        jax.ShapeDtypeStruct((own, F_IN), BF16),
        jax.ShapeDtypeStruct((F_IN, F_HID), F32),
        jax.ShapeDtypeStruct((1, F_HID), F32),
    )
    arrays = (features, weight, bias.reshape(1, -1), edge_pos, edge_weight, grad_out)
    piece = (pu or ud) + 1
    results = pl.pallas_call(
        functools.partial(kernel, n_src, n_dst, slots, edges),
        out_shape=tuple(pltpu.VMEM(o.shape, o.dtype) for o in outs),
        in_specs=[sm, sm, *[hbm] * 6],
        out_specs=(vm,) * 4,
        scratch_shapes=[
            *[pltpu.VMEM(a.shape, a.dtype) for a in arrays[1:]],
            pltpu.VMEM((n_dst, TILE, F_IN), BF16),
            pltpu.VMEM((n_src * TILE, eb), BF16),
            pltpu.VMEM((n_dst * TILE, eb), BF16),
            pltpu.VMEM((group, edges, TILE), BF16),
            pltpu.VMEM((group, edges, TILE), BF16),
            pltpu.VMEM((eb, F_IN), BF16),
            pltpu.VMEM((n_src if many else 1, TILE, F_IN), F32),
            pltpu.VMEM((n_dst if many else 1, TILE, F_IN), F32),
            pltpu.VMEM((F_HID, F_IN), BF16),
            pltpu.VMEM((n_src, TILE, F_IN), BF16),
            pltpu.VMEM((n_src, TILE, F_IN), BF16),
            pltpu.VMEM((n_src, TILE, F_IN), BF16),
            pltpu.VMEM((n_dst, TILE, F_IN), BF16),
            pltpu.VMEM((n_dst, TILE, F_IN), BF16),
            pltpu.VMEM((n_dst, (ud + 2) * 8, 128), BF16),
            pltpu.VMEM((n_dst, (ud + 2) * 8, 128), BF16),
            pltpu.VMEM((n_src if pu else 1, piece, 8, 128), F32),
            pltpu.VMEM((n_src, piece, 8, 128), F32),
            pltpu.VMEM((n_src, max(pu, 1), 8, 128), F32),
            pltpu.VMEM((n_dst, ud * 8, 128), BF16),
            dma((len(arrays),)),
            *d_sems, *s_sems, *s_sems, *d_sems, *d_sems, *s_sems, *s_sems, *d_sems,
        ],
        compiler_params=pltpu.CompilerParams(
            collective_id=0, has_side_effects=True,
            vmem_limit_bytes=(64 << 20) - (1024 << 10),
        ),
    )(tile_index, edge_count, *arrays)
    hidden, input_grad, weight_grad, bias_grad = pl.pallas_call(
        store,
        out_shape=outs,
        in_specs=[vm] * 4,
        out_specs=(anyw,) * 4,
        scratch_shapes=[dma((4,))],
        compiler_params=pltpu.CompilerParams(vmem_limit_bytes=4 << 20),
    )(*results)
    return hidden, input_grad, weight_grad, bias_grad.reshape(-1)


def solution(mesh):
    placed = (
        P(("src", "dst"), None),
        P(),
        P(),
        P("src", "dst", None),
        P("src", "dst", None),
        P("src", "dst", None, None),
        P("src", "dst", None, None),
        P(("src", "dst"), None),
    )
    return jax.shard_map(
        functools.partial(body, mesh.shape["src"], mesh.shape["dst"]),
        mesh=mesh,
        in_specs=placed,
        out_specs=(P(("src", "dst"), None), P(("src", "dst"), None), P(), P()),
        check_vma=False,
    )
```

```python
import functools
import math

import jax
import jax.numpy as jnp
from jax import lax
from jax.experimental import pallas as pl
from jax.experimental.pallas import tpu as pltpu
from jax.sharding import PartitionSpec as P

TILE = 128
F_IN = 128
F_HID = 256
UNITS = 32
HALF = TILE // 2
F32 = jnp.float32
BF16 = jnp.bfloat16


def flip(me, k):
    out = me
    bit = 1
    while bit <= k:
        if k & bit:
            out = out + bit * (1 - 2 * (lax.div(me, bit) % 2))
        bit *= 2
    return out


def each_peer(n, me, body):
    if n <= 8:
        for k in range(n - 1, 0, -1):
            body(k, flip(me, k))
    else:

        def step(k, carry):
            body(k, lax.rem(me + k, n))
            return carry

        lax.fori_loop(1, n, step, 0)


def rows(i, n=TILE):
    return pl.ds(pl.multiple_of(i * n, n), n)


def kernel(
    n_src, n_dst, slots, edges,
    tid_ref, cnt_ref, x_hbm, w_hbm, b_hbm, pos_hbm, ew_hbm, go_hbm,
    hid_ref, ig_ref, wg_ref, bg_ref,
    w_ref, b_ref, pos_ref, ew_ref, go_ref,
    xs, rt, ct, hot_s, hot_t, picked, facc, bacc, wt, aggs, gps, bsend, brecv, gall, fsend, frecv,
    wsend, drecv, ssend, srecv, wcol, wfin,
    ins, xss, xrs, bss, brs, gss, grs, fss, frs, dss, drs, wss, wrs, css, crs, ass, ars,
):
    me_s = lax.axis_index("src")
    me_d = lax.axis_index("dst")
    ud = UNITS // n_dst
    pu = ud // n_src
    src_peers = functools.partial(each_peer, n_src, me_s)
    dst_peers = functools.partial(each_peer, n_dst, me_d)

    def to_src(s, src, dst, ss, rs):
        return pltpu.make_async_remote_copy(
            src_ref=src, dst_ref=dst, send_sem=ss, recv_sem=rs,
            device_id=(s, me_d), device_id_type=pl.DeviceIdType.MESH,
        )

    def to_dst(d, src, dst, ss, rs):
        return pltpu.make_async_remote_copy(
            src_ref=src, dst_ref=dst, send_sem=ss, recv_sem=rs,
            device_id=(me_s, d), device_id_type=pl.DeviceIdType.MESH,
        )

    def feat(k, d):
        return to_dst(d, x_hbm, xs.at[me_d], xss.at[k], xrs.at[k])

    def part(k, s, h):
        half = pl.ds(h * HALF, HALF)
        return to_src(s, bsend.at[k, half], brecv.at[k, half], bss.at[k, h], brs.at[k, h])

    def back(k, s, h):
        mine = gall.at[me_s, pl.ds(h * HALF, HALF)]
        return to_src(s, mine, mine, gss.at[k, h], grs.at[k, h])

    def fin(k, d):
        return to_dst(d, fsend.at[k], frecv.at[k], fss.at[k], frs.at[k])

    def wdst(k, d):
        return to_dst(d, wsend.at[d], drecv.at[me_d], dss.at[k], drs.at[k])

    def wsrc(k, s):
        return to_src(s, ssend.at[s if pu else 0], srecv.at[me_s], wss.at[k], wrs.at[k])

    def wcolumn(k, s):
        return to_src(s, wcol.at[me_s], wcol.at[me_s], css.at[k], crs.at[k])

    def wall(k, d):
        return to_dst(d, wfin.at[me_d], wfin.at[me_d], ass.at[k], ars.at[k])

    loads = [
        pltpu.make_async_copy(a, b, ins.at[i])
        for i, (a, b) in enumerate((
            (x_hbm, xs.at[me_d]), (pos_hbm, pos_ref), (ew_hbm, ew_ref),
            (w_hbm, w_ref), (b_hbm, b_ref), (go_hbm, go_ref),
        ))
    ]
    for c in loads:
        c.start()

    barrier = pltpu.get_barrier_semaphore()

    def greet_src(k, s):
        pl.semaphore_signal(barrier, inc=1, device_id=(s, me_d), device_id_type=pl.DeviceIdType.MESH)

    def greet_dst(k, d):
        pl.semaphore_signal(barrier, inc=1, device_id=(me_s, d), device_id_type=pl.DeviceIdType.MESH)

    src_peers(greet_src)
    dst_peers(greet_dst)
    pl.semaphore_wait(barrier, n_src + n_dst - 2)

    dst_peers(lambda k, d: feat(k, d).start())

    loads[1].wait()
    loads[2].wait()

    group = math.gcd(slots, 16)
    turns = slots // group
    eb = group * edges
    lane = lax.broadcasted_iota(jnp.int32, (1, edges), 1)

    def group_slots(turn):
        if turns == 1:
            return slice(None)
        return pl.ds(pl.multiple_of(turn * group, group), group)

    def build(turn):
        at = group_slots(turn)
        pos = pos_ref[0, 0, at, :]
        weights = ew_ref[0, 0, at, :].astype(F32)
        across = lax.broadcasted_iota(jnp.int32, (edges, TILE), 1)
        turned = pos.T
        tgt, src, wgt = [], [], []
        for j in range(group):
            t = turn * group + j
            tid = tid_ref[0, 0, t]
            p = pos[j : j + 1, :]
            tgt.append(lax.shift_right_logical(p, 7) + lax.div(tid, n_dst) * TILE)
            src.append((p & 127) + lax.rem(tid, n_dst) * TILE)
            wgt.append(jnp.where(lane < cnt_ref[0, 0, t], weights[j : j + 1, :], 0.0))
            c = turned[:, j : j + 1]
            hot_s[j] = jnp.where((c & 127) == across, 1.0, 0.0).astype(BF16)
            hot_t[j] = jnp.where(lax.shift_right_logical(c, 7) == across, 1.0, 0.0).astype(BF16)
        tgt = jnp.concatenate(tgt, axis=1)
        src = jnp.concatenate(src, axis=1)
        wgt = jnp.concatenate(wgt, axis=1)
        spot = lax.broadcasted_iota(jnp.int32, (TILE, eb), 0)

        def col_hot(c):
            ct[rows(c), :] = jnp.where(spot == src - c * TILE, wgt, 0.0).astype(BF16)

        def row_hot(r):
            rt[rows(r), :] = jnp.where(spot == tgt - r * TILE, wgt, 0.0).astype(BF16)

        for n, f in ((n_src, row_hot), (n_dst, col_hot)):
            if n <= 8:
                for i in range(n):
                    f(i)
            else:
                pl.loop(0, n)(f)

    def gather(turn, hot, table, tile_of):
        for j in range(group):
            i = tile_of(tid_ref[0, 0, turn * group + j])
            block = table[i]
            picked[j * edges : (j + 1) * edges, :] = jnp.dot(
                hot[j], block, preferred_element_type=F32
            ).astype(BF16)

    def spread(hot, i):
        return jnp.dot(hot[rows(i), :], picked[...], preferred_element_type=F32)

    def all_turns(hot, table, tile_of, scatter, acc, n):
        acc[...] = jnp.zeros_like(acc)

        @pl.loop(0, turns)
        def _(turn):
            build(turn)
            gather(turn, hot, table, tile_of)

            @pl.loop(0, n)
            def _(i):
                acc[i] += spread(scatter, i)

    if turns == 1:
        build(0)
    for c in loads[3:]:
        c.wait()
    wt[...] = w_ref[...].astype(F32).T.astype(BF16)
    loads[0].wait()
    dst_peers(lambda k, d: feat(k, d).wait_recv())
    if turns == 1:
        gather(0, hot_s, xs, lambda tid: lax.rem(tid, n_dst))
    else:
        all_turns(hot_s, xs, lambda tid: lax.rem(tid, n_dst), rt, facc, n_src)

    def partial_rows(s, h):
        if turns > 1:
            return facc[s, h * HALF : (h + 1) * HALF, :]
        at = pl.ds(pl.multiple_of(s * TILE + h * HALF, HALF), HALF)
        return jnp.dot(rt[at, :], picked[...], preferred_element_type=F32)

    for h in range(2):

        def send_part(k, s, h=h):
            bsend[k, h * HALF : (h + 1) * HALF, :] = partial_rows(s, h).astype(BF16)
            part(k, s, h).start()

        src_peers(send_part)

    for h in range(2):
        half = slice(h * HALF, (h + 1) * HALF)
        agg = partial_rows(me_s, h)
        if n_src <= 8:
            for k in range(1, n_src):
                part(k, flip(me_s, k), h).wait_recv()
                agg = agg + brecv[k, half, :].astype(F32)
        else:

            def take(k, a, h=h, half=half):
                part(k, lax.rem(me_s + k, n_src), h).wait_recv()
                return a + brecv[k, half, :].astype(F32)

            agg = lax.fori_loop(1, n_src, take, agg)
        agg = agg.astype(BF16)
        aggs[half, :] = agg
        preact = jnp.dot(agg, w_ref[...], preferred_element_type=F32) + b_ref[...]
        sig = jax.nn.sigmoid(preact)
        gp = (go_ref[half, :].astype(F32) * sig * (1.0 + preact * (1.0 - sig))).astype(BF16)
        gps[half, :] = gp
        gall[me_s, half, :] = jnp.dot(gp, wt[...], preferred_element_type=F32).astype(BF16)
        src_peers(lambda k, s, h=h: back(k, s, h).start())
        hid_ref[half, :] = (preact * sig).astype(BF16)

    agg, gp = aggs[...], gps[...]
    dw = jnp.dot(agg.astype(F32).T.astype(BF16), gp, preferred_element_type=F32)
    bs = jnp.sum(gp.astype(F32), axis=0, keepdims=True)
    sub = lax.broadcasted_iota(jnp.int32, (8, 128), 0)
    bv = jnp.where(sub == 0, bs[:, :128], jnp.where(sub == 1, bs[:, 128:], 0.0))
    units = []
    for q in range(UNITS):
        i, h = q // 2, q % 2
        units.append(dw[8 * i : 8 * i + 8, 128 * h : 128 * h + 128])
    for d in range(n_dst):
        chunk = jnp.concatenate(units[d * ud : d * ud + ud] + [bv, jnp.zeros_like(bv)], axis=0)
        wsend[d] = chunk.astype(BF16)
    drecv[me_d] = wsend[me_d]
    dst_peers(lambda k, d: wdst(k, d).start())

    def ordered(ref, n):
        total = ref[0].astype(F32)
        for i in range(1, n):
            total = total + ref[i].astype(F32)
        return total

    scale = 1.0 / math.sqrt(TILE * n_src * n_dst)
    dst_peers(lambda k, d: wdst(k, d).wait_recv())
    chunk = ordered(drecv, n_dst).reshape(ud + 2, 8, 128)[: ud + 1]
    if pu:
        for s in range(n_src):
            ssend[s, :pu] = chunk[s * pu : s * pu + pu]
            ssend[s, pu] = chunk[ud]
        srecv[me_s] = ssend[me_s]
    else:
        ssend[0] = chunk
        srecv[me_s] = chunk
    src_peers(lambda k, s: wsrc(k, s).start())
    for h in range(2):
        src_peers(lambda k, s, h=h: back(k, s, h).wait_recv())

    if turns == 1:
        gather(0, hot_t, gall, lambda tid: lax.div(tid, n_dst))
    else:
        all_turns(hot_t, gall, lambda tid: lax.div(tid, n_dst), ct, bacc, n_dst)

    def back_rows(d):
        return spread(ct, d) if turns == 1 else bacc[d]

    def send_fin(k, d):
        fsend[k] = back_rows(d).astype(BF16)
        fin(k, d).start()

    dst_peers(send_fin)

    src_peers(lambda k, s: wsrc(k, s).wait_recv())
    total = ordered(srecv, n_src) * scale
    if pu:
        wcol[me_s] = total[:pu]
        src_peers(lambda k, s: wcolumn(k, s).start())
    own = back_rows(me_d)

    if pu:
        src_peers(lambda k, s: wcolumn(k, s).wait_recv())
        wfin[me_d] = wcol[...].reshape(ud * 8, 128).astype(BF16)
    else:
        wfin[me_d] = total[:ud].reshape(ud * 8, 128).astype(BF16)
    dst_peers(lambda k, d: wall(k, d).start())
    last = -1
    bg_ref[:, :128] = total[last, 0:1, :]
    bg_ref[:, 128:] = total[last, 1:2, :]

    for k in range(n_dst - 1, 0, -1):
        fin(k, me_d).wait_recv()
        own = own + frecv[k].astype(F32)
    ig_ref[...] = own.astype(BF16)

    dst_peers(lambda k, d: wall(k, d).wait_recv())
    for q in range(UNITS):
        i, h = q // 2, q % 2
        at = 8 * (q % ud)
        wg_ref[8 * i : 8 * i + 8, 128 * h : 128 * h + 128] = wfin[q // ud, at : at + 8, :].astype(F32)

    for c in (part, back):
        for h in range(2):
            src_peers(lambda k, p, c=c, h=h: c(k, p, h).wait_send())
    src_copies = (wsrc, wcolumn) if pu else (wsrc,)
    for c in (feat, fin, wdst, wall):
        dst_peers(lambda k, p, c=c: c(k, p).wait_send())
    for c in src_copies:
        src_peers(lambda k, p, c=c: c(k, p).wait_send())


def store(h_in, i_in, w_in, b_in, h_out, i_out, w_out, b_out, sems):
    pairs = ((h_in, h_out), (i_in, i_out), (w_in, w_out), (b_in, b_out))
    copies = [pltpu.make_async_copy(a, b, sems.at[i]) for i, (a, b) in enumerate(pairs)]
    for c in copies:
        c.start()
    for c in copies:
        c.wait()


def body(n_src, n_dst, features, weight, bias, tile_index, edge_count, edge_pos, edge_weight, grad_out):
    slots, edges = edge_pos.shape[2], edge_pos.shape[3]
    own = features.shape[0]
    group = math.gcd(slots, 16)
    eb = group * edges
    many = slots > group
    ud = UNITS // n_dst
    pu = ud // n_src
    vm = pl.BlockSpec(memory_space=pltpu.VMEM)
    sm = pl.BlockSpec(memory_space=pltpu.SMEM)
    hbm = pl.BlockSpec(memory_space=pltpu.HBM)
    anyw = pl.BlockSpec(memory_space=pl.ANY)
    dma = pltpu.SemaphoreType.DMA
    s_sems = [dma((n_src,)), dma((n_src,))]
    h_sems = [dma((n_src, 2)), dma((n_src, 2))]
    d_sems = [dma((n_dst,)), dma((n_dst,))]
    outs = (
        jax.ShapeDtypeStruct((own, F_HID), BF16),
        jax.ShapeDtypeStruct((own, F_IN), BF16),
        jax.ShapeDtypeStruct((F_IN, F_HID), F32),
        jax.ShapeDtypeStruct((1, F_HID), F32),
    )
    arrays = (features, weight, bias.reshape(1, -1), edge_pos, edge_weight, grad_out)
    piece = (pu or ud) + 1
    results = pl.pallas_call(
        functools.partial(kernel, n_src, n_dst, slots, edges),
        out_shape=tuple(pltpu.VMEM(o.shape, o.dtype) for o in outs),
        in_specs=[sm, sm, *[hbm] * 6],
        out_specs=(vm,) * 4,
        scratch_shapes=[
            *[pltpu.VMEM(a.shape, a.dtype) for a in arrays[1:]],
            pltpu.VMEM((n_dst, TILE, F_IN), BF16),
            pltpu.VMEM((n_src * TILE, eb), BF16),
            pltpu.VMEM((n_dst * TILE, eb), BF16),
            pltpu.VMEM((group, edges, TILE), BF16),
            pltpu.VMEM((group, edges, TILE), BF16),
            pltpu.VMEM((eb, F_IN), BF16),
            pltpu.VMEM((n_src if many else 1, TILE, F_IN), F32),
            pltpu.VMEM((n_dst if many else 1, TILE, F_IN), F32),
            pltpu.VMEM((F_HID, F_IN), BF16),
            pltpu.VMEM((TILE, F_IN), BF16),
            pltpu.VMEM((TILE, F_HID), BF16),
            pltpu.VMEM((n_src, TILE, F_IN), BF16),
            pltpu.VMEM((n_src, TILE, F_IN), BF16),
            pltpu.VMEM((n_src, TILE, F_IN), BF16),
            pltpu.VMEM((n_dst, TILE, F_IN), BF16),
            pltpu.VMEM((n_dst, TILE, F_IN), BF16),
            pltpu.VMEM((n_dst, (ud + 2) * 8, 128), BF16),
            pltpu.VMEM((n_dst, (ud + 2) * 8, 128), BF16),
            pltpu.VMEM((n_src if pu else 1, piece, 8, 128), F32),
            pltpu.VMEM((n_src, piece, 8, 128), F32),
            pltpu.VMEM((n_src, max(pu, 1), 8, 128), F32),
            pltpu.VMEM((n_dst, ud * 8, 128), BF16),
            dma((len(arrays),)),
            *d_sems, *h_sems, *h_sems, *d_sems, *d_sems, *s_sems, *s_sems, *d_sems,
        ],
        compiler_params=pltpu.CompilerParams(
            collective_id=0, has_side_effects=True,
            vmem_limit_bytes=(64 << 20) - (1024 << 10),
        ),
    )(tile_index, edge_count, *arrays)
    hidden, input_grad, weight_grad, bias_grad = pl.pallas_call(
        store,
        out_shape=outs,
        in_specs=[vm] * 4,
        out_specs=(anyw,) * 4,
        scratch_shapes=[dma((4,))],
        compiler_params=pltpu.CompilerParams(vmem_limit_bytes=4 << 20),
    )(*results)
    return hidden, input_grad, weight_grad, bias_grad.reshape(-1)


def solution(mesh):
    placed = (
        P(("src", "dst"), None),
        P(),
        P(),
        P("src", "dst", None),
        P("src", "dst", None),
        P("src", "dst", None, None),
        P("src", "dst", None, None),
        P(("src", "dst"), None),
    )
    return jax.shard_map(
        functools.partial(body, mesh.shape["src"], mesh.shape["dst"]),
        mesh=mesh,
        in_specs=placed,
        out_specs=(P(("src", "dst"), None), P(("src", "dst"), None), P(), P()),
        check_vma=False,
    )
```

```python
import functools
import math

import jax
import jax.numpy as jnp
from jax import lax
from jax.experimental import pallas as pl
from jax.experimental.pallas import tpu as pltpu
from jax.sharding import PartitionSpec as P

TILE = 128
F_IN = 128
F_HID = 256
UNITS = 32
F32 = jnp.float32
BF16 = jnp.bfloat16


def flip(me, k):
    out = me
    bit = 1
    while bit <= k:
        if k & bit:
            out = out + bit * (1 - 2 * (lax.div(me, bit) % 2))
        bit *= 2
    return out


def each_peer(n, me, body):
    if n <= 8:
        for k in range(n - 1, 0, -1):
            body(k, flip(me, k))
    else:

        def step(k, carry):
            body(k, lax.rem(me + k, n))
            return carry

        lax.fori_loop(1, n, step, 0)


def rows(i, n=TILE):
    return pl.ds(pl.multiple_of(i * n, n), n)


def kernel(
    n_src, n_dst, slots, edges,
    tid_ref, cnt_ref, x_hbm, w_hbm, b_hbm, pos_hbm, ew_hbm, go_hbm,
    hid_ref, ig_ref, wg_ref, bg_ref,
    w_ref, b_ref, pos_ref, ew_ref, go_ref,
    xs, rt, ct, hot_s, hot_t, picked, facc, bacc, wt, bsend, brecv, gall, fsend, frecv,
    wsend, drecv, srecv, wfin,
    ins, xss, xrs, bss, brs, gss, grs, fss, frs, dss, drs, wss, wrs, ass, ars,
):
    me_s = lax.axis_index("src")
    me_d = lax.axis_index("dst")
    ud = UNITS // n_dst
    src_peers = functools.partial(each_peer, n_src, me_s)
    dst_peers = functools.partial(each_peer, n_dst, me_d)

    def to_src(s, src, dst, ss, rs):
        return pltpu.make_async_remote_copy(
            src_ref=src, dst_ref=dst, send_sem=ss, recv_sem=rs,
            device_id=(s, me_d), device_id_type=pl.DeviceIdType.MESH,
        )

    def to_dst(d, src, dst, ss, rs):
        return pltpu.make_async_remote_copy(
            src_ref=src, dst_ref=dst, send_sem=ss, recv_sem=rs,
            device_id=(me_s, d), device_id_type=pl.DeviceIdType.MESH,
        )

    def feat(k, d):
        return to_dst(d, x_hbm, xs.at[me_d], xss.at[k], xrs.at[k])

    def part(k, s):
        return to_src(s, bsend.at[k], brecv.at[k], bss.at[k], brs.at[k])

    def back(k, s):
        return to_src(s, gall.at[me_s], gall.at[me_s], gss.at[k], grs.at[k])

    def fin(k, d):
        return to_dst(d, fsend.at[k], frecv.at[k], fss.at[k], frs.at[k])

    def wdst(k, d):
        return to_dst(d, wsend.at[d], drecv.at[me_d], dss.at[k], drs.at[k])

    def wsrc(k, s):
        return to_src(s, srecv.at[me_s], srecv.at[me_s], wss.at[k], wrs.at[k])

    def wall(k, d):
        return to_dst(d, wfin.at[me_d], wfin.at[me_d], ass.at[k], ars.at[k])

    loads = [
        pltpu.make_async_copy(a, b, ins.at[i])
        for i, (a, b) in enumerate((
            (x_hbm, xs.at[me_d]), (pos_hbm, pos_ref), (ew_hbm, ew_ref),
            (w_hbm, w_ref), (b_hbm, b_ref), (go_hbm, go_ref),
        ))
    ]
    for c in loads:
        c.start()

    barrier = pltpu.get_barrier_semaphore()

    def greet_src(k, s):
        pl.semaphore_signal(barrier, inc=1, device_id=(s, me_d), device_id_type=pl.DeviceIdType.MESH)

    def greet_dst(k, d):
        pl.semaphore_signal(barrier, inc=1, device_id=(me_s, d), device_id_type=pl.DeviceIdType.MESH)

    src_peers(greet_src)
    dst_peers(greet_dst)
    pl.semaphore_wait(barrier, n_src + n_dst - 2)

    dst_peers(lambda k, d: feat(k, d).start())

    loads[1].wait()
    loads[2].wait()

    group = math.gcd(slots, 16)
    turns = slots // group
    eb = group * edges
    lane = lax.broadcasted_iota(jnp.int32, (1, edges), 1)

    def group_slots(turn):
        if turns == 1:
            return slice(None)
        return pl.ds(pl.multiple_of(turn * group, group), group)

    def build(turn):
        at = group_slots(turn)
        pos = pos_ref[0, 0, at, :]
        weights = ew_ref[0, 0, at, :].astype(F32)
        across = lax.broadcasted_iota(jnp.int32, (edges, TILE), 1)
        turned = pos.T
        tgt, src, wgt = [], [], []
        for j in range(group):
            t = turn * group + j
            tid = tid_ref[0, 0, t]
            p = pos[j : j + 1, :]
            tgt.append(lax.shift_right_logical(p, 7) + lax.div(tid, n_dst) * TILE)
            src.append((p & 127) + lax.rem(tid, n_dst) * TILE)
            wgt.append(jnp.where(lane < cnt_ref[0, 0, t], weights[j : j + 1, :], 0.0))
            c = turned[:, j : j + 1]
            hot_s[j] = jnp.where((c & 127) == across, 1.0, 0.0).astype(BF16)
            hot_t[j] = jnp.where(lax.shift_right_logical(c, 7) == across, 1.0, 0.0).astype(BF16)
        tgt = jnp.concatenate(tgt, axis=1)
        src = jnp.concatenate(src, axis=1)
        wgt = jnp.concatenate(wgt, axis=1)
        spot = lax.broadcasted_iota(jnp.int32, (TILE, eb), 0)

        def col_hot(c):
            ct[rows(c), :] = jnp.where(spot == src - c * TILE, wgt, 0.0).astype(BF16)

        def row_hot(r):
            rt[rows(r), :] = jnp.where(spot == tgt - r * TILE, wgt, 0.0).astype(BF16)

        for n, f in ((n_src, row_hot), (n_dst, col_hot)):
            if n <= 8:
                for i in range(n):
                    f(i)
            else:
                pl.loop(0, n)(f)

    def gather(turn, hot, table, tile_of):
        for j in range(group):
            i = tile_of(tid_ref[0, 0, turn * group + j])
            block = table[i]
            picked[j * edges : (j + 1) * edges, :] = jnp.dot(
                hot[j], block, preferred_element_type=F32
            ).astype(BF16)

    def spread(hot, i):
        return jnp.dot(hot[rows(i), :], picked[...], preferred_element_type=F32)

    def all_turns(hot, table, tile_of, scatter, acc, n):
        acc[...] = jnp.zeros_like(acc)

        @pl.loop(0, turns)
        def _(turn):
            build(turn)
            gather(turn, hot, table, tile_of)

            @pl.loop(0, n)
            def _(i):
                acc[i] += spread(scatter, i)

    if turns == 1:
        build(0)
    for c in loads[3:]:
        c.wait()
    wt[...] = w_ref[...].astype(F32).T.astype(BF16)
    loads[0].wait()
    dst_peers(lambda k, d: feat(k, d).wait_recv())
    if turns == 1:
        gather(0, hot_s, xs, lambda tid: lax.rem(tid, n_dst))
    else:
        all_turns(hot_s, xs, lambda tid: lax.rem(tid, n_dst), rt, facc, n_src)

    def partial_rows(s):
        return spread(rt, s) if turns == 1 else facc[s]

    def send_part(k, s):
        bsend[k] = partial_rows(s).astype(BF16)
        part(k, s).start()

    src_peers(send_part)
    agg = partial_rows(me_s)
    if n_src <= 8:
        for k in range(1, n_src):
            part(k, flip(me_s, k)).wait_recv()
            agg = agg + brecv[k].astype(F32)
    else:

        def take(k, a):
            part(k, lax.rem(me_s + k, n_src)).wait_recv()
            return a + brecv[k].astype(F32)

        agg = lax.fori_loop(1, n_src, take, agg)
    agg = agg.astype(BF16)

    preact = jnp.dot(agg, w_ref[...], preferred_element_type=F32) + b_ref[...]
    sig = jax.nn.sigmoid(preact)
    gp = (go_ref[...].astype(F32) * sig * (1.0 + preact * (1.0 - sig))).astype(BF16)
    gall[me_s] = jnp.dot(gp, wt[...], preferred_element_type=F32).astype(BF16)
    src_peers(lambda k, s: back(k, s).start())
    hid_ref[...] = (preact * sig).astype(BF16)

    dw = jnp.dot(agg.astype(F32).T.astype(BF16), gp, preferred_element_type=F32)
    bs = jnp.sum(gp.astype(F32), axis=0, keepdims=True)
    sub = lax.broadcasted_iota(jnp.int32, (8, 128), 0)
    bv = jnp.where(sub == 0, bs[:, :128], jnp.where(sub == 1, bs[:, 128:], 0.0))
    units = []
    for q in range(UNITS):
        i, h = q // 2, q % 2
        units.append(dw[8 * i : 8 * i + 8, 128 * h : 128 * h + 128])
    for d in range(n_dst):
        chunk = jnp.concatenate(units[d * ud : d * ud + ud] + [bv, jnp.zeros_like(bv)], axis=0)
        wsend[d] = chunk.astype(BF16)
    drecv[me_d] = wsend[me_d]
    dst_peers(lambda k, d: wdst(k, d).start())

    def ordered(ref, n):
        total = ref[0].astype(F32)
        for i in range(1, n):
            total = total + ref[i].astype(F32)
        return total

    scale = 1.0 / math.sqrt(TILE * n_src * n_dst)
    dst_peers(lambda k, d: wdst(k, d).wait_recv())
    srecv[me_s] = ordered(drecv, n_dst).astype(BF16)
    src_peers(lambda k, s: wsrc(k, s).start())
    src_peers(lambda k, s: back(k, s).wait_recv())

    if turns == 1:
        gather(0, hot_t, gall, lambda tid: lax.div(tid, n_dst))
    else:
        all_turns(hot_t, gall, lambda tid: lax.div(tid, n_dst), ct, bacc, n_dst)

    def back_rows(d):
        return spread(ct, d) if turns == 1 else bacc[d]

    def send_fin(k, d):
        fsend[k] = back_rows(d).astype(BF16)
        fin(k, d).start()

    dst_peers(send_fin)

    src_peers(lambda k, s: wsrc(k, s).wait_recv())
    total = ordered(srecv, n_src) * scale
    own = back_rows(me_d)

    wfin[me_d] = total[: ud * 8].astype(BF16)
    dst_peers(lambda k, d: wall(k, d).start())
    bg_ref[:, :128] = total[ud * 8 : ud * 8 + 1, :]
    bg_ref[:, 128:] = total[ud * 8 + 1 : ud * 8 + 2, :]

    for k in range(n_dst - 1, 0, -1):
        fin(k, me_d).wait_recv()
        own = own + frecv[k].astype(F32)
    ig_ref[...] = own.astype(BF16)

    dst_peers(lambda k, d: wall(k, d).wait_recv())
    for q in range(UNITS):
        i, h = q // 2, q % 2
        at = 8 * (q % ud)
        wg_ref[8 * i : 8 * i + 8, 128 * h : 128 * h + 128] = wfin[q // ud, at : at + 8, :].astype(F32)

    src_copies = (part, back, wsrc)
    for c in (feat, fin, wdst, wall):
        dst_peers(lambda k, p, c=c: c(k, p).wait_send())
    for c in src_copies:
        src_peers(lambda k, p, c=c: c(k, p).wait_send())


def store(h_in, i_in, w_in, b_in, h_out, i_out, w_out, b_out, sems):
    pairs = ((h_in, h_out), (i_in, i_out), (w_in, w_out), (b_in, b_out))
    copies = [pltpu.make_async_copy(a, b, sems.at[i]) for i, (a, b) in enumerate(pairs)]
    for c in copies:
        c.start()
    for c in copies:
        c.wait()


def body(n_src, n_dst, features, weight, bias, tile_index, edge_count, edge_pos, edge_weight, grad_out):
    slots, edges = edge_pos.shape[2], edge_pos.shape[3]
    own = features.shape[0]
    group = math.gcd(slots, 16)
    eb = group * edges
    many = slots > group
    ud = UNITS // n_dst
    vm = pl.BlockSpec(memory_space=pltpu.VMEM)
    sm = pl.BlockSpec(memory_space=pltpu.SMEM)
    hbm = pl.BlockSpec(memory_space=pltpu.HBM)
    anyw = pl.BlockSpec(memory_space=pl.ANY)
    dma = pltpu.SemaphoreType.DMA
    s_sems = [dma((n_src,)), dma((n_src,))]
    d_sems = [dma((n_dst,)), dma((n_dst,))]
    outs = (
        jax.ShapeDtypeStruct((own, F_HID), BF16),
        jax.ShapeDtypeStruct((own, F_IN), BF16),
        jax.ShapeDtypeStruct((F_IN, F_HID), F32),
        jax.ShapeDtypeStruct((1, F_HID), F32),
    )
    arrays = (features, weight, bias.reshape(1, -1), edge_pos, edge_weight, grad_out)
    results = pl.pallas_call(
        functools.partial(kernel, n_src, n_dst, slots, edges),
        out_shape=tuple(pltpu.VMEM(o.shape, o.dtype) for o in outs),
        in_specs=[sm, sm, *[hbm] * 6],
        out_specs=(vm,) * 4,
        scratch_shapes=[
            *[pltpu.VMEM(a.shape, a.dtype) for a in arrays[1:]],
            pltpu.VMEM((n_dst, TILE, F_IN), BF16),
            pltpu.VMEM((n_src * TILE, eb), BF16),
            pltpu.VMEM((n_dst * TILE, eb), BF16),
            pltpu.VMEM((group, edges, TILE), BF16),
            pltpu.VMEM((group, edges, TILE), BF16),
            pltpu.VMEM((eb, F_IN), BF16),
            pltpu.VMEM((n_src if many else 1, TILE, F_IN), F32),
            pltpu.VMEM((n_dst if many else 1, TILE, F_IN), F32),
            pltpu.VMEM((F_HID, F_IN), BF16),
            pltpu.VMEM((n_src, TILE, F_IN), BF16),
            pltpu.VMEM((n_src, TILE, F_IN), BF16),
            pltpu.VMEM((n_src, TILE, F_IN), BF16),
            pltpu.VMEM((n_dst, TILE, F_IN), BF16),
            pltpu.VMEM((n_dst, TILE, F_IN), BF16),
            pltpu.VMEM((n_dst, (ud + 2) * 8, 128), BF16),
            pltpu.VMEM((n_dst, (ud + 2) * 8, 128), BF16),
            pltpu.VMEM((n_src, (ud + 2) * 8, 128), BF16),
            pltpu.VMEM((n_dst, ud * 8, 128), BF16),
            dma((len(arrays),)),
            *d_sems, *s_sems, *s_sems, *d_sems, *d_sems, *s_sems, *d_sems,
        ],
        compiler_params=pltpu.CompilerParams(
            collective_id=0, has_side_effects=True,
            vmem_limit_bytes=(64 << 20) - (1024 << 10),
        ),
    )(tile_index, edge_count, *arrays)
    hidden, input_grad, weight_grad, bias_grad = pl.pallas_call(
        store,
        out_shape=outs,
        in_specs=[vm] * 4,
        out_specs=(anyw,) * 4,
        scratch_shapes=[dma((4,))],
        compiler_params=pltpu.CompilerParams(vmem_limit_bytes=4 << 20),
    )(*results)
    return hidden, input_grad, weight_grad, bias_grad.reshape(-1)


def solution(mesh):
    placed = (
        P(("src", "dst"), None),
        P(),
        P(),
        P("src", "dst", None),
        P("src", "dst", None),
        P("src", "dst", None, None),
        P("src", "dst", None, None),
        P(("src", "dst"), None),
    )
    return jax.shard_map(
        functools.partial(body, mesh.shape["src"], mesh.shape["dst"]),
        mesh=mesh,
        in_specs=placed,
        out_specs=(P(("src", "dst"), None), P(("src", "dst"), None), P(), P()),
        check_vma=False,
    )
```
